128 devices in a mesh: row: 8 (over y, core), col: 16 (over x, z).
Axes of the slice: x: 4, y: 4, z: 4, core: 2. Of those that a mesh axis runs over, the one named last changes fastest.
Arguments:
- object_field: float32 [2, 8192, 8192], P(None, 'row', 'col'), may hold values from -6 to 6
- probe_modes: float32 [2, 2, 256, 256], replicated, may hold values from -3 to 3
- measured: float32 [1536, 256, 256], P(('row', 'col')), may hold values from 0.25 to 8
- offsets: int32 [2, 1536], P(None, ('row', 'col')), may hold values from 0 to 7936, as said below
- live_slots: int32 [1536], P(('row', 'col')), may hold values from 0 to 1, as said below
Outputs:
- new_object: float32 [2, 8192, 8192], P(None, 'row', 'col')
- new_probe: float32 [2, 2, 256, 256], replicated
The draws below stay inside these ranges and needn't reach their ends.
Inputs may be any that keep to these rules, and one draw needn't show every extreme that they name: Slot s belongs to device d = s // 12, at mesh position (d // 16, d % 16) = (r, c). Its window's top-left corner lies in that device's tile: r * 1024 <= offsets[0, s] < (r + 1) * 1024 and c * 512 <= offsets[1, s] < (c + 1) * 512; the window lies inside the object: offsets[0, s] <= 7936, offsets[1, s] <= 7936. `live_slots`: on each device the live slots come first; every device has at least one, and some device has all 12.
All inputs are finite; a program needn't handle non-finite values.
Results may differ from the reference program's by a relative error of at most 0.0059.
Values sent between devices are 32-bit elements; how exact they have to be, the bound alone decides.
No kernel may reach another device: no remote copies, remote signals or barrier semaphores. Data moves between devices by JAX's collectives and lax.ppermute only.
A program may use at most 256 MiB of HBM per device.

```python
import math
import jax
import jax.numpy as jnp
from jax import lax

M = 256
MODES = 2
TILE_R = 1024
TILE_C = 512
POS_DEV = 12
NY = 8192
NX = 8192
SLOTS = 1536
N_ROW = 8
N_COL = 16


def draw_offsets(key, part):
    key = jax.random.fold_in(key, 11)
    key_rows, key_cols = jax.random.split(key)
    devices = N_ROW * N_COL
    slot_ids = jnp.arange(SLOTS, dtype=jnp.int32)
    device_ids = slot_ids // POS_DEV
    row_ids = device_ids // N_COL
    col_ids = device_ids % N_COL
    row_span = jnp.where(row_ids == N_ROW - 1, TILE_R - M + 1, TILE_R)
    col_span = jnp.where(col_ids == N_COL - 1, TILE_C - M + 1, TILE_C)
    row_at = row_ids * TILE_R + jax.random.randint(key_rows, (SLOTS,), 0, row_span)
    col_at = col_ids * TILE_C + jax.random.randint(key_cols, (SLOTS,), 0, col_span)
    last_slot = (devices - 1) * POS_DEV
    row_at = jnp.where(slot_ids == 0, 0, jnp.where(slot_ids == last_slot, NY - M, row_at))
    col_at = jnp.where(slot_ids == 0, 0, jnp.where(slot_ids == last_slot, NX - M, col_at))
    return jnp.stack([row_at, col_at]).astype(jnp.int32)


def draw_live_slots(key, part):
    key = jax.random.fold_in(key, 23)
    key_counts, key_full = jax.random.split(key)
    devices = N_ROW * N_COL
    counts = jax.random.randint(key_counts, (devices,), (POS_DEV + 2) // 3, POS_DEV + 1)
    full_device = jax.random.randint(key_full, (), 0, devices)
    counts = jnp.where(jnp.arange(devices, dtype=jnp.int32) == full_device, POS_DEV, counts)
    slot_ids = jnp.arange(SLOTS, dtype=jnp.int32)
    return (slot_ids % POS_DEV < counts[slot_ids // POS_DEV]).astype(jnp.int32)


def shard_levels(rng, extent, pieces, least, top_value):
    factor_of, own = 1.0, jax.random.fold_in(rng, 6)
    for axis_at, parts in pieces:
        steps = jnp.exp(jax.random.uniform(jax.random.fold_in(own, axis_at), (parts,), jnp.float32, least / len(pieces), top_value / len(pieces)))
        factor_of = factor_of * jnp.repeat(steps, extent[axis_at] // parts).reshape([-1 if axis == axis_at else 1 for axis in range(len(extent))])
    return factor_of


def noise(own_key, shape, width, bound, cuts=(), held_as=jnp.bfloat16):
    drawn = jax.random.normal(own_key, shape, jnp.float32) * width
    if len(cuts) > 0:
        drawn = shard_levels(own_key, shape, cuts, -0.22, 0.18) * drawn
    return jnp.clip(drawn, min=-bound, max=bound).astype(held_as)


def setup_inputs(seed: int = 0) -> dict:
    key_of = jax.random.split(jax.random.key(seed), 6)
    object_field = noise(key_of[0], (2, NY, NX), 1.0, 6.0, ((1, 8), (2, 16)), jnp.float32)
    probe_modes = noise(key_of[1], (2, MODES, M, M), 0.5, 3.0, (), jnp.float32)
    measured = jnp.clip(jnp.exp(math.log(8.0) - 3.465736 * jax.random.uniform(key_of[2], (SLOTS, M, M), jnp.float32) ** shard_levels(key_of[2], (SLOTS, M, M), ((0, 128),), -0.2, 0.2)), 0.25, 8.0)
    offsets = draw_offsets(jax.random.fold_in(key_of[5], 71), 0)
    live_slots = draw_live_slots(jax.random.fold_in(key_of[5], 71), 0)
    return {"object_field": object_field, "probe_modes": probe_modes, "measured": measured, "offsets": offsets, "live_slots": live_slots}


def dft_tables(length):
    indices = jnp.arange(length, dtype=jnp.int32)
    product = indices[:, None] * indices[None, :] % length
    angles = product.astype(jnp.float32) * (2.0 * math.pi / length)
    norm_scale = 1.0 / math.sqrt(length)
    return ((jnp.cos(angles) * norm_scale).astype(jnp.bfloat16), (-jnp.sin(angles) * norm_scale).astype(jnp.bfloat16))

def left_mul(mat_re, mat_im, data_re, data_im):
    mat_re = mat_re.astype(jnp.float32)
    mat_im = mat_im.astype(jnp.float32)
    data_re = data_re.astype(jnp.float32)
    data_im = data_im.astype(jnp.float32)
    out_re = jnp.einsum('ab,kbc->kac', mat_re, data_re) - jnp.einsum('ab,kbc->kac', mat_im, data_im)
    out_im = jnp.einsum('ab,kbc->kac', mat_re, data_im) + jnp.einsum('ab,kbc->kac', mat_im, data_re)
    return (out_re, out_im)

def right_mul(data_re, data_im, mat_re, mat_im):
    mat_re = mat_re.astype(jnp.float32)
    mat_im = mat_im.astype(jnp.float32)
    data_re = data_re.astype(jnp.float32)
    data_im = data_im.astype(jnp.float32)
    out_re = jnp.einsum('kab,bc->kac', data_re, mat_re) - jnp.einsum('kab,bc->kac', data_im, mat_im)
    out_im = jnp.einsum('kab,bc->kac', data_re, mat_im) + jnp.einsum('kab,bc->kac', data_im, mat_re)
    return (out_re, out_im)

def wave_terms(patch_re, patch_im, probe_modes, measured_one, table_re, table_im):
    probe_re = probe_modes[0]
    probe_im = probe_modes[1]
    exit_re = (probe_re * patch_re - probe_im * patch_im).astype(jnp.bfloat16)
    exit_im = (probe_re * patch_im + probe_im * patch_re).astype(jnp.bfloat16)
    half_re, half_im = left_mul(table_re, table_im, exit_re, exit_im)
    far_re, far_im = right_mul(half_re.astype(jnp.bfloat16), half_im.astype(jnp.bfloat16), table_re, table_im)
    intensity = lax.optimization_barrier(jnp.sum(far_re * far_re + far_im * far_im, axis=0))
    factor = 1.0 - jnp.sqrt(measured_one) / jnp.sqrt(jnp.maximum(intensity, 0.25))
    resid_re = (far_re * factor).astype(jnp.bfloat16)
    resid_im = (far_im * factor).astype(jnp.bfloat16)
    back_re, back_im = left_mul(table_re, -table_im, resid_re, resid_im)
    return right_mul(back_re.astype(jnp.bfloat16), back_im.astype(jnp.bfloat16), table_re, -table_im)

def reference(object_field, probe_modes, measured, offsets, live_slots):
    table_re, table_im = dft_tables(M)
    probe_re = probe_modes[0]
    probe_im = probe_modes[1]
    lighting = lax.optimization_barrier(jnp.sum(probe_re * probe_re + probe_im * probe_im, axis=0))

    def visit(carry, item):
        accumulated, probe_sum, coverage = carry
        row_at, col_at, weight, measured_one = item
        zero_at = row_at * 0
        patch = lax.dynamic_slice(object_field, (zero_at, row_at, col_at), (2, M, M))
        patch_re = patch[0]
        patch_im = patch[1]
        near_re, near_im = wave_terms(patch_re, patch_im, probe_modes, measured_one, table_re, table_im)
        weight_f = weight.astype(jnp.float32)
        obj_re = lax.optimization_barrier(jnp.sum(probe_re * near_re + probe_im * near_im, axis=0))
        obj_im = lax.optimization_barrier(jnp.sum(probe_re * near_im - probe_im * near_re, axis=0))
        update = jnp.stack([obj_re, obj_im, lighting]) * weight_f
        current = lax.dynamic_slice(accumulated, (zero_at, row_at, col_at), (3, M, M))
        accumulated = lax.dynamic_update_slice(accumulated, current + update, (zero_at, row_at, col_at))
        term = jnp.stack([patch_re * near_re + patch_im * near_im, patch_re * near_im - patch_im * near_re])
        probe_sum = probe_sum + weight_f * term
        coverage = coverage + weight_f * (patch_re * patch_re + patch_im * patch_im)
        return ((accumulated, probe_sum, coverage), None)
    start = (jnp.zeros((3, NY, NX), jnp.float32), jnp.zeros((2, MODES, M, M), jnp.float32), jnp.zeros((M, M), jnp.float32))
    (accumulated, probe_sum, coverage), _ = lax.scan(visit, start, (offsets[0], offsets[1], live_slots, measured))
    new_object = object_field - accumulated[0:2] / jnp.sqrt(accumulated[2:3] + 1.0)
    new_probe = probe_modes - probe_sum / jnp.sqrt(coverage + 1.0)
    return (new_object, new_probe)
```

```python
import functools
import math

import jax
import jax.numpy as jnp
import ml_dtypes
import numpy as np
from jax import lax
from jax.experimental import pallas as pl
from jax.experimental.pallas import tpu as pltpu
from jax.sharding import PartitionSpec as P

M = 256
BOTH = ("row", "col")


def dft_tables(length):
    indices = np.arange(length)
    angles = (indices[:, None] * indices[None, :] % length) * (2.0 * math.pi / length)
    scale = 1.0 / math.sqrt(length)
    real = (np.cos(angles) * scale).astype(np.float32).astype(ml_dtypes.bfloat16)
    imag = (-np.sin(angles) * scale).astype(np.float32).astype(ml_dtypes.bfloat16)
    plain = np.block([[real, -imag], [imag, real]])
    conj = np.block([[real, imag], [-imag, real]])
    return plain, conj


def shifted(value, axis, steps):
    count = lax.axis_size(axis)
    first, last = (max(0, -steps), min(count, count - steps))
    return lax.ppermute(value, axis, [(source, source + steps) for source in range(first, last)])


def shifted_both(value, steps):
    rows, cols = lax.axis_size("row"), lax.axis_size("col")
    pairs = []
    for r in range(rows):
        for c in range(cols):
            if 0 <= r + steps < rows and 0 <= c + steps < cols:
                pairs.append((r * cols + c, (r + steps) * cols + c + steps))
    return lax.ppermute(value, BOTH, pairs)


def cut_strip(ref, channel, row_base, row_rest, col_base, col_rest, rows):
    lane = lax.broadcasted_iota(jnp.int32, (rows + 8, 128), 1)
    keep = lane < 128 - col_rest
    turn = (128 - col_rest) & 127
    tiles = [
        pltpu.roll(ref[channel, pl.ds(row_base, rows + 8), pl.ds(col_base + 128 * t, 128)], turn, 1)
        for t in range(3)
    ]
    groups = rows // 8
    sub = lax.broadcasted_iota(jnp.int32, (groups, 8, 128), 1)
    keep_rows = sub < 8 - row_rest
    turn_rows = (8 - row_rest) & 7
    out = []
    for t in range(2):
        joined = jnp.where(keep, tiles[t], tiles[t + 1]).reshape(groups + 1, 8, 128)
        turned = pltpu.roll(joined, turn_rows, 1)
        out.append(jnp.where(keep_rows, turned[:groups], turned[1:]).reshape(rows, 128))
    return jnp.concatenate(out, axis=1)


def add_strip(ref, channel, row_base, row_rest, col_base, col_rest, value):
    rows = value.shape[0]
    groups = rows // 8
    sub = lax.broadcasted_iota(jnp.int32, (groups, 8, 128), 1)
    keep_rows = sub >= row_rest
    lane = lax.broadcasted_iota(jnp.int32, (rows + 8, 128), 1)
    keep = lane >= col_rest
    halves = []
    for t in range(2):
        turned = pltpu.roll(value[:, 128 * t : 128 * (t + 1)].reshape(groups, 8, 128), row_rest, 1)
        upper = jnp.where(keep_rows, turned, 0.0)
        lower = turned - upper
        zero = jnp.zeros((1, 8, 128), jnp.float32)
        full = jnp.concatenate([upper, zero], 0) + jnp.concatenate([zero, lower], 0)
        halves.append(pltpu.roll(full.reshape(rows + 8, 128), col_rest, 1))
    zero = jnp.zeros_like(halves[0])
    parts = [
        jnp.where(keep, halves[0], zero),
        jnp.where(keep, halves[1], halves[0]),
        jnp.where(keep, zero, halves[1]),
    ]
    for t in range(3):
        at = (channel, pl.ds(row_base, rows + 8), pl.ds(col_base + 128 * t, 128))
        ref[at] = ref[at] + parts[t]


def split_at(index, step):
    base = (index // step) * step
    return pl.multiple_of(base, step), index - base


STRIP = 32


def wave_kernel(
    meta, tile, right, lower, corner, measured, probe, plain, conj,
    own_out, right_out, lower_out, corner_out, sums,
    ext, acc, meas, patch, wave, half, far, in_sem, meas_sem, out_sem,
):
    tr, tc = tile.shape[1], tile.shape[2]
    live = meta[2, 0]
    for t in range(1, meta.shape[1]):
        live = live + meta[2, t]
    loads = [
        pltpu.make_async_copy(tile, ext.at[:, :tr, :tc], in_sem.at[0]),
        pltpu.make_async_copy(right, ext.at[:, :tr, tc:], in_sem.at[1]),
        pltpu.make_async_copy(lower, ext.at[:, tr:, :tc], in_sem.at[2]),
        pltpu.make_async_copy(corner, ext.at[:, tr:, tc:], in_sem.at[3]),
    ]
    for copy in loads:
        copy.start()

    def fetch(slot):
        return pltpu.make_async_copy(measured.at[slot], meas.at[slot], meas_sem.at[slot])

    def start_fetch(slot, carry):
        fetch(slot).start()
        return carry

    lax.fori_loop(0, live, start_fetch, 0)

    def clear(at, carry):
        acc[:, pl.ds(pl.multiple_of(at * 32, 32), 32), :] = jnp.zeros((2, 32, acc.shape[2]), jnp.float32)
        return carry

    lax.fori_loop(0, acc.shape[1] // 32, clear, 0)
    sums[...] = jnp.zeros_like(sums)
    for copy in loads:
        copy.wait()

    def visit(slot, carry):
        row_base, row_rest = split_at(meta[0, slot], 8)
        col_base, col_rest = split_at(meta[1, slot], 128)
        for at in range(0, M, STRIP):
            rows = pl.ds(at, STRIP)
            base = pl.multiple_of(row_base + at, 8)
            o_re = cut_strip(ext, 0, base, row_rest, col_base, col_rest, STRIP)
            o_im = cut_strip(ext, 1, base, row_rest, col_base, col_rest, STRIP)
            patch[0, rows, :] = o_re
            patch[1, rows, :] = o_im
            sums[4, rows, :] += o_re * o_re + o_im * o_im
            for k in range(2):
                p_re = probe[0, k, rows, :]
                p_im = probe[1, k, rows, :]
                cols = pl.ds(M * k, M)
                wave[rows, cols] = (p_re * o_re - p_im * o_im).astype(jnp.bfloat16)
                wave[pl.ds(M + at, STRIP), cols] = (p_re * o_im + p_im * o_re).astype(jnp.bfloat16)

        def left(table):
            for k in range(2):
                for part in range(2):
                    half[M * k : M * (k + 1), M * part : M * (part + 1)] = jnp.dot(
                        table[M * part : M * (part + 1), :],
                        wave[:, M * k : M * (k + 1)],
                        preferred_element_type=jnp.float32,
                    ).astype(jnp.bfloat16)

        def right_mul(table):
            for k in range(2):
                for part in range(2):
                    far[M * k : M * (k + 1), M * part : M * (part + 1)] = jnp.dot(
                        half[M * k : M * (k + 1), :],
                        table[:, M * part : M * (part + 1)],
                        preferred_element_type=jnp.float32,
                    )

        left(plain)
        right_mul(conj)
        fetch(slot).wait()
        for at in range(0, M, STRIP):
            rows = pl.ds(at, STRIP)
            parts = [
                [far[pl.ds(M * k + at, STRIP), M * part : M * (part + 1)] for part in range(2)]
                for k in range(2)
            ]
            intensity = parts[0][0] * parts[0][0] + parts[0][1] * parts[0][1]
            intensity = intensity + parts[1][0] * parts[1][0] + parts[1][1] * parts[1][1]
            level = meas[slot, rows, :]
            factor = 1.0 - level * lax.rsqrt(level * jnp.maximum(intensity, 0.25))
            for k in range(2):
                for part in range(2):
                    wave[pl.ds(M * part + at, STRIP), M * k : M * (k + 1)] = (
                        parts[k][part] * factor
                    ).astype(jnp.bfloat16)
        left(conj)
        right_mul(plain)
        for at in range(0, M, STRIP):
            rows = pl.ds(at, STRIP)
            base = pl.multiple_of(row_base + at, 8)
            o_re = patch[0, rows, :]
            o_im = patch[1, rows, :]
            g_re = None
            for k in range(2):
                n_re = far[pl.ds(M * k + at, STRIP), :M]
                n_im = far[pl.ds(M * k + at, STRIP), M:]
                p_re = probe[0, k, rows, :]
                p_im = probe[1, k, rows, :]
                sums[k, rows, :] += o_re * n_re + o_im * n_im
                sums[2 + k, rows, :] += o_re * n_im - o_im * n_re
                t_re = p_re * n_re + p_im * n_im
                t_im = p_re * n_im - p_im * n_re
                g_re, g_im = (t_re, t_im) if g_re is None else (g_re + t_re, g_im + t_im)
            add_strip(acc, 0, base, row_rest, col_base, col_rest, g_re)
            add_strip(acc, 1, base, row_rest, col_base, col_rest, g_im)
        return carry

    lax.fori_loop(0, live, visit, 0)
    stores = [
        pltpu.make_async_copy(acc.at[:, :tr, :tc], own_out, out_sem.at[0]),
        pltpu.make_async_copy(acc.at[:, :tr, tc:], right_out, out_sem.at[1]),
        pltpu.make_async_copy(acc.at[:, tr:, :tc], lower_out, out_sem.at[2]),
        pltpu.make_async_copy(acc.at[:, tr:, tc:], corner_out, out_sem.at[3]),
    ]
    for copy in stores:
        copy.start()
    for copy in stores:
        copy.wait()


def run_waves(meta, tile, right, lower, corner, measured, probe, plain, conj):
    slots = measured.shape[0]
    tr, tc = tile.shape[1], tile.shape[2]
    f32 = jnp.float32
    anywhere = pl.BlockSpec(memory_space=pl.ANY)
    vmem = pl.BlockSpec(memory_space=pltpu.VMEM)
    return pl.pallas_call(
        wave_kernel,
        out_shape=[
            jax.ShapeDtypeStruct((2, tr, tc), f32),
            jax.ShapeDtypeStruct((2, tr, M), f32),
            jax.ShapeDtypeStruct((2, M, tc), f32),
            jax.ShapeDtypeStruct((2, M, M), f32),
            jax.ShapeDtypeStruct((5, M, M), f32),
        ],
        in_specs=[pl.BlockSpec(memory_space=pltpu.SMEM)] + [anywhere] * 5 + [vmem] * 3,
        out_specs=[anywhere] * 4 + [vmem],
        scratch_shapes=[
            pltpu.VMEM((2, tr + M, tc + M), f32),
            pltpu.VMEM((2, tr + M, tc + M), f32),
            pltpu.VMEM((slots, M, M), f32),
            pltpu.VMEM((2, M, M), f32),
            pltpu.VMEM((2 * M, 2 * M), jnp.bfloat16),
            pltpu.VMEM((2 * M, 2 * M), jnp.bfloat16),
            pltpu.VMEM((2 * M, 2 * M), f32),
            pltpu.SemaphoreType.DMA((4,)),
            pltpu.SemaphoreType.DMA((slots,)),
            pltpu.SemaphoreType.DMA((4,)),
        ],
        compiler_params=pltpu.CompilerParams(vmem_limit_bytes=40 * 1024 * 1024),
        cost_estimate=pl.CostEstimate(
            flops=2 * slots * 32 * M**3, bytes_accessed=24 * 2**20, transcendentals=0
        ),
    )(meta, tile, right, lower, corner, measured, probe, plain, conj)


def light_kernel(meta, probe, scale, light):
    slots = meta.shape[1]
    rows, cols = scale.shape
    light[...] = jnp.zeros_like(light)

    def visit(slot, carry):
        row, col = meta[0, slot], meta[1, slot]
        seen = (meta[2, slot] > 0) & (row > -M) & (row < rows) & (col > -M) & (col < cols)

        @pl.when(seen)
        def _():
            row_base, row_rest = split_at(row + M, 8)
            col_base, col_rest = split_at(col + M, 128)
            for at in range(0, M, STRIP):
                here = pl.ds(at, STRIP)
                value = probe[0, 0, here, :] * probe[0, 0, here, :]
                for part, k in ((1, 0), (0, 1), (1, 1)):
                    value = value + probe[part, k, here, :] * probe[part, k, here, :]
                base = pl.multiple_of(row_base + at, 8)
                add_strip(light, 0, base, row_rest, col_base, col_rest, value)

        return carry

    lax.fori_loop(0, slots, visit, 0)
    for at in range(0, rows, 64):
        scale[at : at + 64, :] = lax.rsqrt(light[0, M + at : M + at + 64, M : M + cols] + 1.0)


def run_light(meta, probe, rows, cols):
    return pl.pallas_call(
        light_kernel,
        out_shape=jax.ShapeDtypeStruct((rows, cols), jnp.float32),
        in_specs=[
            pl.BlockSpec(memory_space=pltpu.SMEM),
            pl.BlockSpec(memory_space=pltpu.VMEM),
        ],
        out_specs=pl.BlockSpec(memory_space=pltpu.VMEM),
        scratch_shapes=[pltpu.VMEM((1, rows + 2 * M, cols + 2 * M), jnp.float32)],
        compiler_params=pltpu.CompilerParams(vmem_limit_bytes=24 * 1024 * 1024),
        cost_estimate=pl.CostEstimate(flops=10**8, bytes_accessed=24 * 2**20, transcendentals=0),
    )(meta, probe)


def finish_kernel(tile, own, side, below, corner, scale, out):
    step = pl.program_id(0)
    total = own[...]
    cols = out.shape[2]
    factor = scale[...][None]
    out[:, :, M:] = tile[:, :, M:] - total[:, :, M:] * factor[:, :, M:]
    out[:, :, :M] = tile[:, :, :M] - (total[:, :, :M] + side[...]) * factor[:, :, :M]

    @pl.when(step == 0)
    def _():
        out[...] = out[...] - below[...] * factor
        out[:, :, :M] = out[:, :, :M] - corner[...] * factor[:, :, :M]


def run_finish(tile, own, side, below, corner, scale):
    rows, cols = tile.shape[1], tile.shape[2]
    block = pl.BlockSpec((2, M, cols), lambda i: (0, i, 0))
    return pl.pallas_call(
        finish_kernel,
        grid=(rows // M,),
        out_shape=jax.ShapeDtypeStruct(tile.shape, jnp.float32),
        in_specs=[
            block,
            block,
            pl.BlockSpec((2, M, M), lambda i: (0, i, 0)),
            pl.BlockSpec((2, M, cols), lambda i: (0, 0, 0)),
            pl.BlockSpec((2, M, M), lambda i: (0, 0, 0)),
            pl.BlockSpec((M, cols), lambda i: (i, 0)),
        ],
        out_specs=block,
        compiler_params=pltpu.CompilerParams(vmem_limit_bytes=24 * 1024 * 1024),
        cost_estimate=pl.CostEstimate(flops=10**7, bytes_accessed=20 * 2**20, transcendentals=0),
    )(tile, own, side, below, corner, scale)


STAGES = (("row", 1, 2), ("col", 1, 4), ("col", 4, 4), ("row", 2, 4))


def place(stage):
    axis, stride, length = stage
    return (lax.axis_index(axis) // stride) % length


def turned(value, stage, steps):
    axis, stride, length = stage
    pairs = []
    for source in range(lax.axis_size(axis)):
        at = (source // stride) % length
        pairs.append((source, source + ((at + steps) % length - at) * stride))
    return lax.ppermute(value, axis, pairs)


def piece_of(value, stage, steps):
    length = stage[2]
    rows = value.shape[1] // length
    at = (place(stage) + steps) % length
    return lax.dynamic_slice_in_dim(value, at * rows, rows, 1)


def scatter_sum(value):
    for stage in STAGES:
        sent = [piece_of(value, stage, steps) for steps in range(stage[2])]
        got = [turned(sent[steps], stage, steps) for steps in range(1, stage[2])]
        value = functools.reduce(jnp.add, got, sent[0])
    return value


def take_piece(value):
    for stage in STAGES:
        value = piece_of(value, stage, 0)
    return value


def gather_pieces(value):
    for stage in STAGES[::-1]:
        length, rows = stage[2], value.shape[1]
        parts = [value] + [turned(value, stage, steps) for steps in range(1, length)]
        whole = jnp.zeros((value.shape[0], length * rows) + value.shape[2:], value.dtype)
        for steps, part in enumerate(parts):
            at = (place(stage) - steps) % length
            whole = lax.dynamic_update_slice_in_dim(whole, part, at * rows, 1)
        value = whole
    return value


def on_device(object_field, probe_modes, measured, offsets, live_slots):
    rows, cols = object_field.shape[1], object_field.shape[2]
    plain, conj = (jnp.asarray(table) for table in dft_tables(M))
    right = shifted(object_field[:, :, :M], "col", -1)
    lower = shifted(object_field[:, :M, :], "row", -1)
    corner = shifted_both(object_field[:, :M, :M], -1)
    meta = jnp.concatenate(
        [
            offsets[0:1] - lax.axis_index("row") * rows,
            offsets[1:2] - lax.axis_index("col") * cols,
            live_slots[None],
        ],
        axis=0,
    )
    left_meta = shifted(meta, "col", 1) - jnp.array([[0], [cols], [0]], jnp.int32)
    wide_meta = jnp.concatenate([meta, left_meta], axis=1)
    upper_meta = shifted(wide_meta, "row", 1) - jnp.array([[rows], [0], [0]], jnp.int32)
    scale = run_light(jnp.concatenate([wide_meta, upper_meta], axis=1), probe_modes, rows, cols)
    own, side, below, diag, sums = run_waves(
        meta, object_field, right, lower, corner, measured, probe_modes, plain, conj
    )
    side = shifted(side, "col", 1)
    below = shifted(below, "row", 1)
    diag = shifted_both(diag, 1)
    piece = scatter_sum(sums.reshape(5, M * 2, 128))
    mine = take_piece(probe_modes.reshape(4, M * 2, 128))
    mine = mine - piece[:4] / jnp.sqrt(piece[4:5] + 1.0)
    new_probe = gather_pieces(mine).reshape(2, 2, M, M)
    new_object = run_finish(object_field, own, side, below, diag, scale)
    return (new_object, new_probe)


def solution(mesh):
    placed = (
        P(None, "row", "col"),
        P(),
        P(("row", "col"), None, None),
        P(None, ("row", "col")),
        P(("row", "col")),
    )
    return jax.shard_map(
        on_device,
        mesh=mesh,
        in_specs=placed,
        out_specs=(P(None, "row", "col"), P()),
        check_vma=False,
    )
```

```python
import functools
import math

import jax
import jax.numpy as jnp
import ml_dtypes
import numpy as np
from jax import lax
from jax.experimental import pallas as pl
from jax.experimental.pallas import tpu as pltpu
from jax.sharding import Mesh
from jax.sharding import PartitionSpec as P

M = 256


def dft_tables(length):
    indices = np.arange(length)
    angles = (indices[:, None] * indices[None, :] % length) * (2.0 * math.pi / length)
    scale = 1.0 / math.sqrt(length)
    real = (np.cos(angles) * scale).astype(np.float32).astype(ml_dtypes.bfloat16)
    imag = (-np.sin(angles) * scale).astype(np.float32).astype(ml_dtypes.bfloat16)
    plain = np.block([[real, -imag], [imag, real]])
    conj = np.block([[real, imag], [-imag, real]])
    return plain, conj


def shifted(value, axis, steps):
    count = lax.axis_size(axis)
    first, last = (max(0, -steps), min(count, count - steps))
    return lax.ppermute(value, axis, [(source, source + steps) for source in range(first, last)])


def shifted_both(value, steps):
    rows, cols = lax.axis_size(ROW), lax.axis_size(COL)
    pairs = []
    for r in range(rows):
        for c in range(cols):
            if 0 <= r + steps < rows and 0 <= c + steps < cols:
                pairs.append((r * cols + c, (r + steps) * cols + c + steps))
    return lax.ppermute(value, ROW + COL, pairs)


def cut_strip(ref, channel, row_base, row_rest, col_base, col_rest, rows):
    lane = lax.broadcasted_iota(jnp.int32, (rows + 8, 128), 1)
    keep = lane < 128 - col_rest
    turn = (128 - col_rest) & 127
    tiles = [
        pltpu.roll(ref[channel, pl.ds(row_base, rows + 8), pl.ds(col_base + 128 * t, 128)], turn, 1)
        for t in range(3)
    ]
    groups = rows // 8
    sub = lax.broadcasted_iota(jnp.int32, (groups, 8, 128), 1)
    keep_rows = sub < 8 - row_rest
    turn_rows = (8 - row_rest) & 7
    out = []
    for t in range(2):
        joined = jnp.where(keep, tiles[t], tiles[t + 1]).reshape(groups + 1, 8, 128)
        turned = pltpu.roll(joined, turn_rows, 1)
        out.append(jnp.where(keep_rows, turned[:groups], turned[1:]).reshape(rows, 128))
    return jnp.concatenate(out, axis=1)


def add_strip(ref, channel, row_base, row_rest, col_base, col_rest, value):
    rows = value.shape[0]
    groups = rows // 8
    sub = lax.broadcasted_iota(jnp.int32, (groups, 8, 128), 1)
    keep_rows = sub >= row_rest
    lane = lax.broadcasted_iota(jnp.int32, (rows + 8, 128), 1)
    keep = lane >= col_rest
    halves = []
    for t in range(2):
        turned = pltpu.roll(value[:, 128 * t : 128 * (t + 1)].reshape(groups, 8, 128), row_rest, 1)
        upper = jnp.where(keep_rows, turned, 0.0)
        lower = turned - upper
        zero = jnp.zeros((1, 8, 128), jnp.float32)
        full = jnp.concatenate([upper, zero], 0) + jnp.concatenate([zero, lower], 0)
        halves.append(pltpu.roll(full.reshape(rows + 8, 128), col_rest, 1))
    zero = jnp.zeros_like(halves[0])
    parts = [
        jnp.where(keep, halves[0], zero),
        jnp.where(keep, halves[1], halves[0]),
        jnp.where(keep, zero, halves[1]),
    ]
    for t in range(3):
        at = (channel, pl.ds(row_base, rows + 8), pl.ds(col_base + 128 * t, 128))
        ref[at] = ref[at] + parts[t]


def split_at(index, step):
    base = (index // step) * step
    return pl.multiple_of(base, step), index - base


STRIP = 32
PIECE = 16


def wave_kernel(plan, meta, core, measured, probe, plain, conj, *refs):
    loads, inits, outs = plan["loads"], plan["inits"], plan["outs"]
    row_at, col_at, height, width = plan["region"]
    refs = list(refs)

    def take(count):
        taken, refs[:] = refs[:count], refs[count:]
        return taken

    load_refs, init_refs = take(len(loads)), take(len(inits))
    before = take(1)[0] if plan["follows"] else None
    take(plan["after"])
    out_refs = take(len(outs))
    sum_refs = take(2 if plan["last"] else 1)
    order, ext, acc, meas, sums, patch, wave, half, far, in_sem, meas_sem, out_sem = refs
    slots = meta.shape[1]

    copies = []

    def copy_in(source, target):
        copy = pltpu.make_async_copy(source, target, in_sem.at[len(copies)])
        copies.append(copy)
        copy.start()

    for (r, c, top, start, h, w), ref in zip(loads, load_refs):
        copy_in(ref.at[:, top : top + h, start : start + w], ext.at[:, r : r + h, c : c + w])

    def fetch(slot):
        return pltpu.make_async_copy(measured.at[slot], meas.at[slot], meas_sem.at[slot])

    count = jnp.int32(0)
    for slot in range(slots):
        row, col, live = meta[0, slot], meta[1, slot], meta[2, slot]
        mine = (live > 0) & (row >= plan["rows"][0]) & (row < plan["rows"][1])
        mine = mine & (col >= plan["cols"][0]) & (col < plan["cols"][1])

        @pl.when(mine)
        def _(slot=slot, count=count):
            order[count] = slot
            fetch(slot).start()

        count = count + mine.astype(jnp.int32)

    for r, c, h, w in plan["clear"]:

        def clear(at, carry, r=r, c=c, w=w):
            rows = pl.ds(pl.multiple_of(r + at * 32, 32), 32)
            acc[:, rows, c : c + w] = jnp.zeros((2, 32, w), jnp.float32)
            return carry

        lax.fori_loop(0, h // 32, clear, 0)
    for (r, c), ref in zip(inits, init_refs):
        copy_in(ref, acc.at[:, r : r + ref.shape[1], c : c + ref.shape[2]])
    if before is None:
        sums[...] = jnp.zeros_like(sums)
    else:
        copy_in(before, sums)
    for copy in copies:
        copy.wait()

    def left(table):
        for k in range(2):
            for part in range(2):
                half[M * k : M * (k + 1), M * part : M * (part + 1)] = jnp.dot(
                    table[M * part : M * (part + 1), :],
                    wave[:, M * k : M * (k + 1)],
                    preferred_element_type=jnp.float32,
                ).astype(jnp.bfloat16)

    def right_mul(table):
        for k in range(2):
            for part in range(2):
                far[M * k : M * (k + 1), M * part : M * (part + 1)] = jnp.dot(
                    half[M * k : M * (k + 1), :],
                    table[:, M * part : M * (part + 1)],
                    preferred_element_type=jnp.float32,
                )

    def add_sum(channel, at, value):
        for row in range(0, STRIP, PIECE):
            block = (at + row) // PIECE
            sums[0, block, channel] += value[row : row + PIECE, :128]
            sums[1, block, channel] += value[row : row + PIECE, 128:]

    def visit(step, carry):
        slot = order[step]
        row_base, row_rest = split_at(meta[0, slot] - row_at, 8)
        col_base, col_rest = split_at(meta[1, slot] - col_at, 128)
        for at in range(0, M, STRIP):
            rows = pl.ds(at, STRIP)
            base = pl.multiple_of(row_base + at, 8)
            o_re = cut_strip(ext, 0, base, row_rest, col_base, col_rest, STRIP)
            o_im = cut_strip(ext, 1, base, row_rest, col_base, col_rest, STRIP)
            patch[0, rows, :] = o_re
            patch[1, rows, :] = o_im
            add_sum(4, at, o_re * o_re + o_im * o_im)
            for k in range(2):
                p_re = probe[0, k, rows, :]
                p_im = probe[1, k, rows, :]
                cols = pl.ds(M * k, M)
                wave[rows, cols] = (p_re * o_re - p_im * o_im).astype(jnp.bfloat16)
                wave[pl.ds(M + at, STRIP), cols] = (p_re * o_im + p_im * o_re).astype(jnp.bfloat16)
        left(plain)
        right_mul(conj)
        fetch(slot).wait()
        for at in range(0, M, STRIP):
            rows = pl.ds(at, STRIP)
            parts = [
                [far[pl.ds(M * k + at, STRIP), M * part : M * (part + 1)] for part in range(2)]
                for k in range(2)
            ]
            intensity = parts[0][0] * parts[0][0] + parts[0][1] * parts[0][1]
            intensity = intensity + parts[1][0] * parts[1][0] + parts[1][1] * parts[1][1]
            level = meas[slot, rows, :]
            factor = 1.0 - level * lax.rsqrt(level * jnp.maximum(intensity, 0.25))
            for k in range(2):
                for part in range(2):
                    wave[pl.ds(M * part + at, STRIP), M * k : M * (k + 1)] = (
                        parts[k][part] * factor
                    ).astype(jnp.bfloat16)
        left(conj)
        right_mul(plain)
        for at in range(0, M, STRIP):
            rows = pl.ds(at, STRIP)
            base = pl.multiple_of(row_base + at, 8)
            o_re = patch[0, rows, :]
            o_im = patch[1, rows, :]
            g_re = None
            for k in range(2):
                n_re = far[pl.ds(M * k + at, STRIP), :M]
                n_im = far[pl.ds(M * k + at, STRIP), M:]
                p_re = probe[0, k, rows, :]
                p_im = probe[1, k, rows, :]
                add_sum(k, at, o_re * n_re + o_im * n_im)
                add_sum(2 + k, at, o_re * n_im - o_im * n_re)
                t_re = p_re * n_re + p_im * n_im
                t_im = p_re * n_im - p_im * n_re
                g_re, g_im = (t_re, t_im) if g_re is None else (g_re + t_re, g_im + t_im)
            add_strip(acc, 0, base, row_rest, col_base, col_rest, g_re)
            add_strip(acc, 1, base, row_rest, col_base, col_rest, g_im)
        return carry

    lax.fori_loop(0, count, visit, 0)
    stores = []
    if plan["last"]:
        stores.append((sums.at[core[0]], sum_refs[0]))
        stores.append((sums.at[1 - core[0]], sum_refs[1]))
    else:
        stores.append((sums, sum_refs[0]))
    for (r, c, h, w), ref in zip(outs, out_refs):
        stores.append((acc.at[:, r : r + h, c : c + w], ref))
    stores = [pltpu.make_async_copy(a, b, out_sem.at[i]) for i, (a, b) in enumerate(stores)]
    for copy in stores:
        copy.start()
    for copy in stores:
        copy.wait()


def run_waves(plan, meta, core, measured, probe, tables, loads, inits, before=None, after=()):
    slots = measured.shape[0]
    height, width = plan["region"][2:]
    f32 = jnp.float32
    plan = dict(
        plan,
        loads=[place for place, _ in loads],
        inits=[place for place, _ in inits],
        follows=before is not None,
        after=len(after),
    )
    anywhere = pl.BlockSpec(memory_space=pl.ANY)
    vmem = pl.BlockSpec(memory_space=pltpu.VMEM)
    smem = pl.BlockSpec(memory_space=pltpu.SMEM)
    arrays = [array for _, array in loads] + [array for _, array in inits]
    arrays = arrays + ([] if before is None else [before]) + list(after)
    shapes = [jax.ShapeDtypeStruct((2, h, w), f32) for _, _, h, w in plan["outs"]]
    if plan["last"]:
        shapes = shapes + [jax.ShapeDtypeStruct((M // PIECE, 5, PIECE, M // 2), f32)] * 2
    else:
        shapes = shapes + [jax.ShapeDtypeStruct((2, M // PIECE, 5, PIECE, M // 2), f32)]
    return pl.pallas_call(
        functools.partial(wave_kernel, plan),
        out_shape=shapes,
        in_specs=[smem, smem, anywhere] + [vmem] * 3 + [anywhere] * len(arrays),
        out_specs=[anywhere] * len(shapes),
        scratch_shapes=[
            pltpu.SMEM((slots,), jnp.int32),
            pltpu.VMEM((2, height, width), f32),
            pltpu.VMEM((2, height, width), f32),
            pltpu.VMEM((slots, M, M), f32),
            pltpu.VMEM((2, M // PIECE, 5, PIECE, M // 2), f32),
            pltpu.VMEM((2, M, M), f32),
            pltpu.VMEM((2 * M, 2 * M), jnp.bfloat16),
            pltpu.VMEM((2 * M, 2 * M), jnp.bfloat16),
            pltpu.VMEM((2 * M, 2 * M), f32),
            pltpu.SemaphoreType.DMA((len(arrays) + 1,)),
            pltpu.SemaphoreType.DMA((slots,)),
            pltpu.SemaphoreType.DMA((len(shapes),)),
        ],
        compiler_params=pltpu.CompilerParams(vmem_limit_bytes=28 * 1024 * 1024),
        cost_estimate=pl.CostEstimate(
            flops=10**8, bytes_accessed=2**20, transcendentals=0
        ),
        name=plan["name"],
    )(meta, core, measured, probe, *tables, *arrays)


def light_kernel(meta, probe, scale, light):
    slots = meta.shape[1]
    rows, cols = scale.shape
    light[...] = jnp.zeros_like(light)

    def visit(slot, carry):
        row, col = meta[0, slot], meta[1, slot]
        seen = (meta[2, slot] > 0) & (row > -M) & (row < rows) & (col > -M) & (col < cols)

        @pl.when(seen)
        def _():
            row_base, row_rest = split_at(row + M, 8)
            col_base, col_rest = split_at(col + M, 128)
            for at in range(0, M, STRIP):
                here = pl.ds(at, STRIP)
                value = probe[0, 0, here, :] * probe[0, 0, here, :]
                for part, k in ((1, 0), (0, 1), (1, 1)):
                    value = value + probe[part, k, here, :] * probe[part, k, here, :]
                base = pl.multiple_of(row_base + at, 8)
                add_strip(light, 0, base, row_rest, col_base, col_rest, value)

        return carry

    lax.fori_loop(0, slots, visit, 0)
    for at in range(0, rows, 64):
        scale[at : at + 64, :] = lax.rsqrt(light[0, M + at : M + at + 64, M : M + cols] + 1.0)


def run_light(meta, probe, rows, cols):
    return pl.pallas_call(
        light_kernel,
        out_shape=jax.ShapeDtypeStruct((rows, cols), jnp.float32),
        in_specs=[
            pl.BlockSpec(memory_space=pltpu.SMEM),
            pl.BlockSpec(memory_space=pltpu.VMEM),
        ],
        out_specs=pl.BlockSpec(memory_space=pltpu.VMEM),
        scratch_shapes=[pltpu.VMEM((1, rows + 2 * M, cols + 2 * M), jnp.float32)],
        compiler_params=pltpu.CompilerParams(vmem_limit_bytes=24 * 1024 * 1024),
        cost_estimate=pl.CostEstimate(flops=10**8, bytes_accessed=24 * 2**20, transcendentals=0),
    )(meta, probe)


def finish_kernel(
    tile, left_own, upper_own, lower_own, upper_side, lower_side, below_left, below_right, corner, scale, out
):
    step = pl.program_id(0)
    half = pl.num_programs(0) // 2
    factor = scale[...][None]

    def write(own, side):
        out[:, :, :M] = tile[:, :, :M] - (left_own[...] + side[...]) * factor[:, :, :M]
        out[:, :, M:] = tile[:, :, M:] - own[...] * factor[:, :, M:]

    @pl.when(step < half)
    def _():
        write(upper_own, upper_side)

    @pl.when(step >= half)
    def _():
        write(lower_own, lower_side)

    @pl.when(step == 0)
    def _():
        out[:, :, :M] = out[:, :, :M] - (below_left[...] + corner[...]) * factor[:, :, :M]
        out[:, :, M:] = out[:, :, M:] - below_right[...] * factor[:, :, M:]


def run_finish(tile, left_own, upper_own, lower_own, upper_side, lower_side, below_left, below_right, corner, scale):
    rows, cols = tile.shape[1], tile.shape[2]
    steps = rows // M
    half = steps // 2
    block = pl.BlockSpec((2, M, cols), lambda i: (0, i, 0))
    upper = pl.BlockSpec((2, M, M), lambda i: (0, jnp.minimum(i, half - 1), 0))
    lower = pl.BlockSpec((2, M, M), lambda i: (0, jnp.maximum(i - half, 0), 0))
    first = pl.BlockSpec((2, M, M), lambda i: (0, 0, 0))
    return pl.pallas_call(
        finish_kernel,
        grid=(steps,),
        out_shape=jax.ShapeDtypeStruct(tile.shape, jnp.float32),
        in_specs=[
            block,
            pl.BlockSpec((2, M, M), lambda i: (0, i, 0)),
            upper,
            lower,
            upper,
            lower,
            first,
            first,
            first,
            pl.BlockSpec((M, cols), lambda i: (i, 0)),
        ],
        out_specs=block,
        compiler_params=pltpu.CompilerParams(vmem_limit_bytes=24 * 1024 * 1024),
        cost_estimate=pl.CostEstimate(flops=10**7, bytes_accessed=20 * 2**20, transcendentals=0),
        name="finish",
    )(tile, left_own, upper_own, lower_own, upper_side, lower_side, below_left, below_right, corner, scale)


def nothing(value, *rest):
    pass


def gate(value, *after):
    anywhere = pl.BlockSpec(memory_space=pl.ANY)
    return pl.pallas_call(
        nothing,
        out_shape=jax.ShapeDtypeStruct(value.shape, value.dtype),
        in_specs=[anywhere] * (1 + len(after)),
        out_specs=anywhere,
        input_output_aliases={0: 0},
        name="gate",
    )(value, *after)


ROW, COL, PLANE = ("y", "core"), ("x", "z"), ("y", "x")


def exchanged(value, axis):
    return lax.all_to_all(value, axis, split_axis=0, concat_axis=0, tiled=True)


def swapped(value):
    return lax.ppermute(value, "core", [(0, 1), (1, 0)])


def all_sum(value, axis):
    count = lax.axis_size(axis)
    others = [
        lax.ppermute(value, axis, [(at, (at + steps) % count) for at in range(count)])
        for steps in range(1, count)
    ]
    return functools.reduce(jnp.add, others, value)


def on_device(object_field, probe_modes, measured, offsets, live_slots):
    rows, cols = object_field.shape[1], object_field.shape[2]
    tables = tuple(jnp.asarray(table) for table in dft_tables(M))
    mid = rows // 2
    cuts = (0, M, mid + M, rows)
    chunks = [
        shifted(object_field[:, a:b, :M], COL, -1) for a, b in zip(cuts[:-1], cuts[1:])
    ]
    lower = shifted(object_field[:, :M, :], ROW, -1)
    corner = shifted(chunks[0], ROW, -1)
    meta = jnp.concatenate(
        [
            offsets[0:1] - lax.axis_index(ROW) * rows,
            offsets[1:2] - lax.axis_index(COL) * cols,
            live_slots[None],
        ],
        axis=0,
    )
    left_meta = shifted(meta, COL, 1) - jnp.array([[0], [cols], [0]], jnp.int32)
    wide_meta = jnp.concatenate([meta, left_meta], axis=1)
    upper_meta = shifted(wide_meta, ROW, 1) - jnp.array([[rows], [0], [0]], jnp.int32)
    scale = run_light(jnp.concatenate([wide_meta, upper_meta], axis=1), probe_modes, rows, cols)
    core = lax.axis_index("core")[None]
    mine = lax.dynamic_slice(
        probe_modes.reshape(4, M, M),
        (0, lax.axis_index(PLANE) * PIECE, core[0] * (M // 2)),
        (4, PIECE, M // 2),
    )
    common = (meta, core, measured, probe_modes, tables)

    plan = dict(
        name="left",
        region=(0, 0, rows + M, cols),
        rows=(0, rows),
        cols=(0, M),
        clear=[(0, 0, rows + M, cols)],
        outs=[(0, 0, rows, M), (0, M, mid + M, M), (mid + M, M, mid, M), (rows, 0, M, M)],
        last=False,
    )
    left_own, upper_init, lower_init, below_left, sums = run_waves(
        plan, *common, [((0, 0, 0, 0, rows, cols), object_field), ((rows, 0, 0, 0, M, cols), lower)], [], after=(scale,)
    )
    plan = dict(
        name="upper",
        region=(0, M, mid + M, cols),
        rows=(0, mid),
        cols=(M, cols),
        clear=[(0, M, mid + M, M)],
        outs=[(0, 0, mid, M), (0, M, mid, M), (mid, 0, M, cols)],
        last=False,
    )
    upper_own, upper_side, middle, sums = run_waves(
        plan,
        *common,
        [
            ((0, 0, 0, M, mid + M, M), object_field),
            ((0, M, 0, 0, M, M), chunks[0]),
            ((M, M, 0, 0, mid, M), chunks[1]),
        ],
        [((0, 0), upper_init)],
        before=sums,
    )
    plan = dict(
        name="lower",
        region=(mid, M, mid + M, cols),
        rows=(mid, rows),
        cols=(M, cols),
        clear=[(M, M, mid, M)],
        outs=[(0, 0, mid, M), (0, M, mid, M), (mid, 0, M, M), (mid, M, M, M)],
        last=True,
    )
    lower_own, lower_side, below_right, diag, kept, sent = run_waves(
        plan,
        *common,
        [
            ((0, 0, mid, M, mid, M), object_field),
            ((0, M, mid - M, 0, M, M), chunks[1]),
            ((M, M, 0, 0, M, M), chunks[2]),
            ((mid, 0, 0, M, M, M), lower),
            ((mid, M, 0, 0, M, M), corner),
        ],
        [((0, 0), middle), ((M, 0), lower_init)],
        before=sums,
    )
    below_left = shifted(below_left, ROW, 1)
    upper_side = shifted(upper_side, COL, 1)
    lower_side = shifted(lower_side, COL, 1)
    below_right = shifted(below_right, ROW, 1)
    total = kept + swapped(sent)
    piece = jnp.sum(exchanged(total, PLANE), axis=0)
    piece = all_sum(gate(piece, lower_side, upper_side), "z")
    diag = shifted_both(gate(diag, piece), 1)
    mine = mine - piece[:4] / jnp.sqrt(piece[4:5] + 1.0)
    whole = exchanged(jnp.broadcast_to(mine[None], (M // PIECE,) + mine.shape), PLANE)
    whole = gate(whole, diag)
    other = swapped(whole)
    first = core[0] == 0
    new_probe = jnp.concatenate(
        [jnp.where(first, whole, other), jnp.where(first, other, whole)], axis=3
    )
    new_probe = jnp.moveaxis(new_probe, 0, 1)
    new_object = run_finish(
        object_field, left_own, upper_own, lower_own, upper_side, lower_side, below_left, below_right, diag, scale
    )
    return (new_object, new_probe.reshape(probe_modes.shape))


def solution(mesh):
    grid = Mesh(mesh.devices.reshape(4, 2, 4, 4), ROW + COL)
    placed = (
        P(None, ROW, COL),
        P(),
        P(ROW + COL, None, None),
        P(None, ROW + COL),
        P(ROW + COL),
    )
    return jax.shard_map(
        on_device,
        mesh=grid,
        in_specs=placed,
        out_specs=(P(None, ROW, COL), P()),
        check_vma=False,
    )
```

```python
import functools
import math

import jax
import jax.numpy as jnp
import ml_dtypes
import numpy as np
from jax import lax
from jax.experimental import pallas as pl
from jax.experimental.pallas import tpu as pltpu
from jax.sharding import Mesh
from jax.sharding import PartitionSpec as P

M = 256
ROOM = 56 * 1024 * 1024


def dft_tables(length):
    indices = np.arange(length)
    angles = (indices[:, None] * indices[None, :] % length) * (2.0 * math.pi / length)
    scale = 1.0 / math.sqrt(length)
    real = (np.cos(angles) * scale).astype(np.float32).astype(ml_dtypes.bfloat16)
    imag = (-np.sin(angles) * scale).astype(np.float32).astype(ml_dtypes.bfloat16)
    plain = np.block([[real, -imag], [imag, real]])
    conj = np.block([[real, imag], [-imag, real]])
    return plain, conj


def shifted(value, axis, steps):
    count = lax.axis_size(axis)
    first, last = (max(0, -steps), min(count, count - steps))
    return lax.ppermute(value, axis, [(source, source + steps) for source in range(first, last)])


def shifted_both(value, steps):
    rows, cols = lax.axis_size(ROW), lax.axis_size(COL)
    pairs = []
    for r in range(rows):
        for c in range(cols):
            if 0 <= r + steps < rows and 0 <= c + steps < cols:
                pairs.append((r * cols + c, (r + steps) * cols + c + steps))
    return lax.ppermute(value, ROW + COL, pairs)


def cut_strip(ref, channel, row_base, row_rest, col_base, col_rest, rows):
    lane = lax.broadcasted_iota(jnp.int32, (rows + 8, 128), 1)
    keep = lane < 128 - col_rest
    turn = (128 - col_rest) & 127
    tiles = [
        pltpu.roll(ref[channel, pl.ds(row_base, rows + 8), pl.ds(col_base + 128 * t, 128)], turn, 1)
        for t in range(3)
    ]
    groups = rows // 8
    sub = lax.broadcasted_iota(jnp.int32, (groups, 8, 128), 1)
    keep_rows = sub < 8 - row_rest
    turn_rows = (8 - row_rest) & 7
    out = []
    for t in range(2):
        joined = jnp.where(keep, tiles[t], tiles[t + 1]).reshape(groups + 1, 8, 128)
        turned = pltpu.roll(joined, turn_rows, 1)
        out.append(jnp.where(keep_rows, turned[:groups], turned[1:]).reshape(rows, 128))
    return jnp.concatenate(out, axis=1)


def add_strip(ref, channel, row_base, row_rest, col_base, col_rest, value):
    rows = value.shape[0]
    groups = rows // 8
    sub = lax.broadcasted_iota(jnp.int32, (groups, 8, 128), 1)
    keep_rows = sub >= row_rest
    lane = lax.broadcasted_iota(jnp.int32, (rows + 8, 128), 1)
    keep = lane >= col_rest
    halves = []
    for t in range(2):
        turned = pltpu.roll(value[:, 128 * t : 128 * (t + 1)].reshape(groups, 8, 128), row_rest, 1)
        upper = jnp.where(keep_rows, turned, 0.0)
        lower = turned - upper
        zero = jnp.zeros((1, 8, 128), jnp.float32)
        full = jnp.concatenate([upper, zero], 0) + jnp.concatenate([zero, lower], 0)
        halves.append(pltpu.roll(full.reshape(rows + 8, 128), col_rest, 1))
    zero = jnp.zeros_like(halves[0])
    parts = [
        jnp.where(keep, halves[0], zero),
        jnp.where(keep, halves[1], halves[0]),
        jnp.where(keep, zero, halves[1]),
    ]
    for t in range(3):
        at = (channel, pl.ds(row_base, rows + 8), pl.ds(col_base + 128 * t, 128))
        ref[at] = ref[at] + parts[t]


def split_at(index, step):
    base = (index // step) * step
    return pl.multiple_of(base, step), index - base


STRIP = 64
PIECE = 16


def wave_kernel(plan, meta, core, measured, probe, plain, conj, *refs):
    loads, inits, outs = plan["loads"], plan["inits"], plan["outs"]
    row_at, col_at, height, width = plan["region"]
    refs = list(refs)

    def take(count):
        taken, refs[:] = refs[:count], refs[count:]
        return taken

    load_refs, init_refs = take(len(loads)), take(len(inits))
    before = take(1)[0] if plan["follows"] else None
    passed = take(plan["passed"])
    take(plan["after"])
    out_refs = take(len(outs))
    sum_refs = take(2 if plan["last"] else 1)
    order, ext, acc, meas, sums, patch, wave, half, far, in_sem, meas_sem, out_sem = refs
    slots = meta.shape[1]

    copies = []

    def copy_in(source, target):
        copy = pltpu.make_async_copy(source, target, in_sem.at[len(copies)])
        copies.append(copy)
        copy.start()

    for (r, c, top, start, h, w), ref in zip(loads, load_refs):
        copy_in(ref.at[:, top : top + h, start : start + w], ext.at[:, r : r + h, c : c + w])

    def fetch(slot):
        return pltpu.make_async_copy(measured.at[slot], meas.at[slot], meas_sem.at[slot])

    count = jnp.int32(0)
    for slot in range(slots):
        row, col, live = meta[0, slot], meta[1, slot], meta[2, slot]
        mine = (live > 0) & (row >= plan["rows"][0]) & (row < plan["rows"][1])
        mine = mine & (col >= plan["cols"][0]) & (col < plan["cols"][1])

        @pl.when(mine)
        def _(slot=slot, count=count):
            order[count] = slot
            fetch(slot).start()

        count = count + mine.astype(jnp.int32)

    for r, c, h, w in plan["clear"]:

        def clear(at, carry, r=r, c=c, w=w):
            rows = pl.ds(pl.multiple_of(r + at * 32, 32), 32)
            acc[:, rows, c : c + w] = jnp.zeros((2, 32, w), jnp.float32)
            return carry

        lax.fori_loop(0, h // 32, clear, 0)
    for (r, c), ref in zip(inits, init_refs):
        copy_in(ref, acc.at[:, r : r + ref.shape[1], c : c + ref.shape[2]])
    if before is None:
        sums[...] = jnp.zeros_like(sums)
    else:
        copy_in(before, sums)
    for copy in copies:
        copy.wait()

    def left(use, table):
        for k in range(2):
            both = jnp.dot(table[...], wave[use, :, M * k : M * (k + 1)], preferred_element_type=jnp.float32)
            half[use, M * k : M * (k + 1), :M] = both[:M].astype(jnp.bfloat16)
            half[use, M * k : M * (k + 1), M:] = both[M:].astype(jnp.bfloat16)

    def right_mul(use, table):
        for part in range(2):
            far[use, :, M * part : M * (part + 1)] = jnp.dot(
                half[use], table[:, M * part : M * (part + 1)], preferred_element_type=jnp.float32
            )

    def add_sum(channel, at, value):
        for row in range(0, STRIP, PIECE):
            block = (at + row) // PIECE
            sums[0, block, channel] += value[row : row + PIECE, :128]
            sums[1, block, channel] += value[row : row + PIECE, 128:]

    def where(step):
        slot = order[step]
        row_base, row_rest = split_at(meta[0, slot] - row_at, 8)
        col_base, col_rest = split_at(meta[1, slot] - col_at, 128)
        return slot, row_base, row_rest, col_base, col_rest

    def cut(use, slot, row_base, row_rest, col_base, col_rest):
        for at in range(0, M, STRIP):
            rows = pl.ds(at, STRIP)
            base = pl.multiple_of(row_base + at, 8)
            o_re = cut_strip(ext, 0, base, row_rest, col_base, col_rest, STRIP)
            o_im = cut_strip(ext, 1, base, row_rest, col_base, col_rest, STRIP)
            patch[use, 0, rows, :] = o_re
            patch[use, 1, rows, :] = o_im
            add_sum(4, at, o_re * o_re + o_im * o_im)
            for k in range(2):
                p_re = probe[0, k, rows, :]
                p_im = probe[1, k, rows, :]
                cols = pl.ds(M * k, M)
                wave[use, rows, cols] = (p_re * o_re - p_im * o_im).astype(jnp.bfloat16)
                wave[use, pl.ds(M + at, STRIP), cols] = (p_re * o_im + p_im * o_re).astype(jnp.bfloat16)

    def resid(use, slot):
        fetch(slot).wait()
        for at in range(0, M, STRIP):
            rows = pl.ds(at, STRIP)
            parts = [
                [far[use, pl.ds(M * k + at, STRIP), M * part : M * (part + 1)] for part in range(2)]
                for k in range(2)
            ]
            intensity = parts[0][0] * parts[0][0] + parts[0][1] * parts[0][1]
            intensity = intensity + parts[1][0] * parts[1][0] + parts[1][1] * parts[1][1]
            level = meas[slot, rows, :]
            factor = 1.0 - level * lax.rsqrt(level * jnp.maximum(intensity, 0.25))
            for k in range(2):
                for part in range(2):
                    wave[use, pl.ds(M * part + at, STRIP), M * k : M * (k + 1)] = (
                        parts[k][part] * factor
                    ).astype(jnp.bfloat16)

    def grad(use, slot, row_base, row_rest, col_base, col_rest):
        for at in range(0, M, STRIP):
            rows = pl.ds(at, STRIP)
            base = pl.multiple_of(row_base + at, 8)
            o_re = patch[use, 0, rows, :]
            o_im = patch[use, 1, rows, :]
            g_re = None
            for k in range(2):
                n_re = far[use, pl.ds(M * k + at, STRIP), :M]
                n_im = far[use, pl.ds(M * k + at, STRIP), M:]
                p_re = probe[0, k, rows, :]
                p_im = probe[1, k, rows, :]
                add_sum(k, at, o_re * n_re + o_im * n_im)
                add_sum(2 + k, at, o_re * n_im - o_im * n_re)
                t_re = p_re * n_re + p_im * n_im
                t_im = p_re * n_im - p_im * n_re
                g_re, g_im = (t_re, t_im) if g_re is None else (g_re + t_re, g_im + t_im)
            add_strip(acc, 0, base, row_rest, col_base, col_rest, g_re)
            add_strip(acc, 1, base, row_rest, col_base, col_rest, g_im)

    def stages(use, step):
        at = where(step)
        return (
            lambda: cut(use, *at),
            lambda: left(use, plain),
            lambda: right_mul(use, conj),
            lambda: resid(use, at[0]),
            lambda: left(use, conj),
            lambda: right_mul(use, plain),
            lambda: grad(use, *at),
        )

    def visit_pair(pair, carry):
        first, second = stages(0, 2 * pair), stages(1, 2 * pair + 1)
        first[0]()
        for ahead, behind in zip(first[1:], second[:-1]):
            ahead()
            behind()
        second[-1]()
        return carry

    lax.fori_loop(0, count // 2, visit_pair, 0)

    @pl.when(count % 2 == 1)
    def _():
        for stage in stages(0, count - 1):
            stage()

    stores = []
    if plan["last"]:
        stores.append((sums.at[core[0]], sum_refs[0]))
        stores.append((sums.at[1 - core[0]], sum_refs[1]))
    else:
        stores.append((sums, sum_refs[0]))
    for (r, c, h, w, _), ref in zip(outs, out_refs):
        stores.append((acc.at[:, r : r + h, c : c + w], ref.at[:, :, ref.shape[2] - w :]))
    for ref in passed:
        stores.append((ref, out_refs[-1].at[:, :, : ref.shape[2]]))
    stores = [pltpu.make_async_copy(a, b, out_sem.at[i]) for i, (a, b) in enumerate(stores)]
    for copy in stores:
        copy.start()
    for copy in stores:
        copy.wait()


def run_waves(plan, meta, core, measured, probe, tables, loads, inits, before=None, passed=(), after=()):
    slots = measured.shape[0]
    height, width = plan["region"][2:]
    f32 = jnp.float32
    plan = dict(
        plan,
        loads=[place for place, _ in loads],
        inits=[place for place, _ in inits],
        follows=before is not None,
        passed=len(passed),
        after=len(after),
    )
    anywhere = pl.BlockSpec(memory_space=pl.ANY)
    vmem = pl.BlockSpec(memory_space=pltpu.VMEM)
    smem = pl.BlockSpec(memory_space=pltpu.SMEM)
    arrays = [array for _, array in loads] + [array for _, array in inits]
    arrays = arrays + ([] if before is None else [before]) + list(passed) + list(after)
    in_hbm = pl.BlockSpec(memory_space=pltpu.HBM)
    array_specs = [in_hbm if array is loads[0][1] else anywhere for array in arrays]
    shapes = [jax.ShapeDtypeStruct((2, h, w), f32) for _, _, h, w, _ in plan["outs"]]
    out_specs = [in_hbm if stays else anywhere for *_, stays in plan["outs"]]
    for array in passed:
        shapes[-1] = jax.ShapeDtypeStruct((2, M, array.shape[2] + shapes[-1].shape[2]), f32)
    if plan["last"]:
        shapes = shapes + [jax.ShapeDtypeStruct((M // PIECE, 5, PIECE, M // 2), f32)] * 2
    else:
        shapes = shapes + [jax.ShapeDtypeStruct((2, M // PIECE, 5, PIECE, M // 2), f32)]
    return pl.pallas_call(
        functools.partial(wave_kernel, plan),
        out_shape=shapes,
        in_specs=[smem, smem, in_hbm] + [vmem] * 3 + array_specs,
        out_specs=out_specs + [anywhere] * (len(shapes) - len(out_specs)),
        scratch_shapes=[
            pltpu.SMEM((slots,), jnp.int32),
            pltpu.VMEM((2, height, width), f32),
            pltpu.VMEM((2, height, width), f32),
            pltpu.VMEM((slots, M, M), f32),
            pltpu.VMEM((2, M // PIECE, 5, PIECE, M // 2), f32),
            pltpu.VMEM((2, 2, M, M), f32),
            pltpu.VMEM((2, 2 * M, 2 * M), jnp.bfloat16),
            pltpu.VMEM((2, 2 * M, 2 * M), jnp.bfloat16),
            pltpu.VMEM((2, 2 * M, 2 * M), f32),
            pltpu.SemaphoreType.DMA((len(arrays) + 1,)),
            pltpu.SemaphoreType.DMA((slots,)),
            pltpu.SemaphoreType.DMA((len(shapes) + 1,)),
        ],
        compiler_params=pltpu.CompilerParams(vmem_limit_bytes=34 * 1024 * 1024),
        cost_estimate=pl.CostEstimate(
            flops=10**8, bytes_accessed=2**20, transcendentals=0
        ),
        name=plan["name"],
    )(meta, core, measured, probe, *tables, *arrays)


def light_kernel(meta, probe, after, scale, light):
    slots = meta.shape[1]
    rows, cols = scale.shape
    light[...] = jnp.zeros_like(light)

    def visit(slot, carry):
        row, col = meta[0, slot], meta[1, slot]
        seen = (meta[2, slot] > 0) & (row > -M) & (row < rows) & (col > -M) & (col < cols)

        @pl.when(seen)
        def _():
            row_base, row_rest = split_at(row + M, 8)
            col_base, col_rest = split_at(col + M, 128)
            for at in range(0, M, STRIP):
                here = pl.ds(at, STRIP)
                value = probe[0, 0, here, :] * probe[0, 0, here, :]
                for part, k in ((1, 0), (0, 1), (1, 1)):
                    value = value + probe[part, k, here, :] * probe[part, k, here, :]
                base = pl.multiple_of(row_base + at, 8)
                add_strip(light, 0, base, row_rest, col_base, col_rest, value)

        return carry

    lax.fori_loop(0, slots, visit, 0)
    for at in range(0, rows, 64):
        scale[at : at + 64, :] = lax.rsqrt(light[0, M + at : M + at + 64, M : M + cols] + 1.0)


def run_light(meta, probe, after, rows, cols):
    return pl.pallas_call(
        light_kernel,
        out_shape=jax.ShapeDtypeStruct((rows, cols), jnp.float32),
        in_specs=[
            pl.BlockSpec(memory_space=pltpu.SMEM),
            pl.BlockSpec(memory_space=pltpu.VMEM),
            pl.BlockSpec(memory_space=pl.ANY),
        ],
        out_specs=pl.BlockSpec(memory_space=pltpu.VMEM),
        scratch_shapes=[pltpu.VMEM((1, rows + 2 * M, cols + 2 * M), jnp.float32)],
        compiler_params=pltpu.CompilerParams(vmem_limit_bytes=20 * 1024 * 1024),
        cost_estimate=pl.CostEstimate(flops=10**8, bytes_accessed=24 * 2**20, transcendentals=0),
        name="light",
    )(meta, probe, after)


def finish_kernel(
    tile, left_own, upper_own, lower_own, first_side, upper_side, lower_side, below, scale, out
):
    step = pl.program_id(0)
    factor = scale[...][None]

    def write(own, side):
        out[:, :, :M] = tile[:, :, :M] - (left_own[...] + side[...]) * factor[:, :, :M]
        out[:, :, M:] = tile[:, :, M:] - own[...] * factor[:, :, M:]

    @pl.when(step == 0)
    def _():
        write(upper_own, first_side)
        out[...] = out[...] - below[...] * factor

    @pl.when(step == 1)
    def _():
        write(upper_own, upper_side)

    @pl.when(step > 1)
    def _():
        write(lower_own, lower_side)


def run_finish(tile, left_own, upper_own, lower_own, first_side, upper_side, lower_side, below, scale):
    rows, cols = tile.shape[1], tile.shape[2]
    steps = rows // M
    half = steps // 2
    block = pl.BlockSpec((2, M, cols), lambda i: (0, i, 0))
    upper = pl.BlockSpec((2, M, M), lambda i: (0, jnp.minimum(i, half - 1), 0))
    lower = pl.BlockSpec((2, M, M), lambda i: (0, jnp.maximum(i - half, 0), 0))
    first = pl.BlockSpec((2, M, M), lambda i: (0, 0, 0))
    return pl.pallas_call(
        finish_kernel,
        grid=(steps,),
        out_shape=jax.ShapeDtypeStruct(tile.shape, jnp.float32),
        in_specs=[
            block,
            pl.BlockSpec((2, M, M), lambda i: (0, i, 0)),
            upper,
            lower,
            first,
            first,
            lower,
            pl.BlockSpec((2, M, cols), lambda i: (0, 0, 0)),
            pl.BlockSpec((M, cols), lambda i: (i, 0)),
        ],
        out_specs=block,
        compiler_params=pltpu.CompilerParams(vmem_limit_bytes=ROOM),
        cost_estimate=pl.CostEstimate(flops=10**7, bytes_accessed=20 * 2**20, transcendentals=0),
        name="finish",
    )(tile, left_own, upper_own, lower_own, first_side, upper_side, lower_side, below, scale)


def cut_kernel(pieces, after, tile, *refs):
    outs, sem = refs[after:-1], refs[-1]
    copies = [
        pltpu.make_async_copy(tile.at[:, r : r + h, :w], out, sem.at[i])
        for i, ((r, h, w), out) in enumerate(zip(pieces, outs))
    ]
    for copy in copies:
        copy.start()
    for copy in copies:
        copy.wait()


def run_cut(tile, pieces, *after):
    anywhere = pl.BlockSpec(memory_space=pl.ANY)
    return pl.pallas_call(
        functools.partial(cut_kernel, pieces, len(after)),
        out_shape=[jax.ShapeDtypeStruct((2, h, w), jnp.float32) for _, h, w in pieces],
        in_specs=[anywhere] * (1 + len(after)),
        out_specs=[pl.BlockSpec(memory_space=pltpu.VMEM)] * len(pieces),
        scratch_shapes=[pltpu.SemaphoreType.DMA((len(pieces),))],
        compiler_params=pltpu.CompilerParams(vmem_limit_bytes=ROOM),
        name="cut",
    )(tile, *after)


def join_kernel(place, mine, other, out):
    y = place[0]
    first = place[1] == 0
    for back in range(mine.shape[0]):
        for x in range(mine.shape[1]):
            row = ((y - back) & 3) * (M // 4) + x * PIECE
            rows = pl.ds(pl.multiple_of(row, PIECE), PIECE)
            for channel in range(4):
                a, b = mine[back, x, channel], other[back, x, channel]
                out[channel, rows, : M // 2] = jnp.where(first, a, b)
                out[channel, rows, M // 2 :] = jnp.where(first, b, a)


def run_join(place, mine, other):
    vmem = pl.BlockSpec(memory_space=pltpu.VMEM)
    return pl.pallas_call(
        join_kernel,
        out_shape=jax.ShapeDtypeStruct((4, M, M), jnp.float32),
        in_specs=[pl.BlockSpec(memory_space=pltpu.SMEM), vmem, vmem],
        out_specs=vmem,
        compiler_params=pltpu.CompilerParams(vmem_limit_bytes=8 * 1024 * 1024),
        name="join",
    )(place, mine, other)


def nothing(value, *rest):
    pass


def gate(value, *after):
    anywhere = pl.BlockSpec(memory_space=pl.ANY)
    return pl.pallas_call(
        nothing,
        out_shape=jax.ShapeDtypeStruct(value.shape, value.dtype),
        in_specs=[anywhere] * (1 + len(after)),
        out_specs=anywhere,
        input_output_aliases={0: 0},
        compiler_params=pltpu.CompilerParams(vmem_limit_bytes=2**20),
        name="gate",
    )(value, *after)


ROW, COL = ("y", "core"), ("x", "z")


def turned(value, axis, steps):
    count = lax.axis_size(axis)
    return lax.ppermute(value, axis, [(at, (at + steps) % count) for at in range(count)])


def swapped(value):
    return turned(value, "core", 1)


def scatter_sum(value, axis):
    count, me = lax.axis_size(axis), lax.axis_index(axis)
    parts = [
        lax.dynamic_index_in_dim(value, (me + steps) % count, 0, keepdims=False)
        for steps in range(count)
    ]
    others = [turned(parts[steps], axis, steps) for steps in range(1, count)]
    return functools.reduce(jnp.add, others, parts[0])


def all_sum(value, axis):
    others = [turned(value, axis, steps) for steps in range(1, lax.axis_size(axis))]
    return functools.reduce(jnp.add, others, value)


def collected(value, axis):
    others = [turned(value, axis, steps) for steps in range(1, lax.axis_size(axis))]
    return jnp.stack([value] + others)


def on_device(object_field, probe_modes, measured, offsets, live_slots):
    rows, cols = object_field.shape[1], object_field.shape[2]
    tables = tuple(jnp.asarray(table) for table in dft_tables(M))
    mid = rows // 2
    meta = jnp.concatenate(
        [
            offsets[0:1] - lax.axis_index(ROW) * rows,
            offsets[1:2] - lax.axis_index(COL) * cols,
            live_slots[None],
        ],
        axis=0,
    )
    first_cols, top_rows = run_cut(object_field, ((0, mid + M, M), (0, M, cols)))
    left_meta = shifted(meta, COL, 1) - jnp.array([[0], [cols], [0]], jnp.int32)
    wide_meta = jnp.concatenate([meta, left_meta], axis=1)
    upper_meta = shifted(wide_meta, ROW, 1) - jnp.array([[rows], [0], [0]], jnp.int32)
    (last_cols,) = run_cut(object_field, ((mid + M, M, M),), left_meta)
    first_cols = shifted(first_cols, COL, -1)
    last_cols = shifted(last_cols, COL, -1)
    lower = shifted(top_rows, ROW, -1)
    core, y, x = (lax.axis_index(axis) for axis in ("core", "y", "x"))
    mine = lax.dynamic_slice(
        probe_modes.reshape(4, M, M),
        (0, y * (M // 4) + x * PIECE, core * (M // 2)),
        (4, PIECE, M // 2),
    )
    common = (meta, core[None], measured, probe_modes, tables)

    plan = dict(
        name="left",
        region=(0, 0, rows + M, cols),
        rows=(0, rows),
        cols=(0, M),
        clear=[(0, 0, rows + M, cols)],
        outs=[
            (0, 0, rows, M, True),
            (0, M, mid + M, M, False),
            (mid + M, M, mid, M, False),
            (rows, 0, M, M, False),
        ],
        last=False,
    )
    left_own, upper_init, lower_init, below_left, sums = run_waves(
        plan,
        *common,
        [((0, 0, 0, 0, rows, cols), object_field), ((rows, 0, 0, 0, M, cols), lower)],
        [],
        after=(upper_meta,),
    )
    corner = shifted(gate(first_cols[:, :M], sums), ROW, -1)
    plan = dict(
        name="upper",
        region=(0, M, mid + M, cols),
        rows=(0, mid),
        cols=(M, cols),
        clear=[(0, M, mid + M, M)],
        outs=[
            (0, 0, mid, M, True),
            (0, M, M, M, False),
            (M, M, M, M, False),
            (mid, 0, M, cols, False),
        ],
        last=False,
    )
    upper_own, first_side, upper_side, middle, sums = run_waves(
        plan,
        *common,
        [
            ((0, 0, 0, M, mid + M, M), object_field),
            ((0, M, 0, 0, mid + M, M), first_cols),
        ],
        [((0, 0), upper_init)],
        before=sums,
    )
    plan = dict(
        name="lower",
        region=(mid, M, mid + M, cols),
        rows=(mid, rows),
        cols=(M, cols),
        clear=[(M, M, mid, M)],
        outs=[(0, 0, mid, M, True), (0, M, mid, M, False), (mid, 0, M, cols, False)],
        last=True,
    )
    lower_own, lower_side, below, kept, sent = run_waves(
        plan,
        *common,
        [
            ((0, 0, mid, M, mid, M), object_field),
            ((0, M, mid, 0, M, M), first_cols),
            ((M, M, 0, 0, M, M), last_cols),
            ((mid, 0, 0, M, M, M), lower),
            ((mid, M, 0, 0, M, M), corner),
        ],
        [((0, 0), middle), ((M, 0), lower_init)],
        before=sums,
        passed=(below_left,),
    )
    upper_side = shifted(upper_side, COL, 1)
    lower_side = shifted(lower_side, COL, 1)
    total = (kept + swapped(gate(sent, upper_side))).reshape(4, 4, 5, PIECE, M // 2)
    piece = scatter_sum(total, "y")
    below = shifted(gate(below, piece), ROW, 1)
    scale = run_light(
        jnp.concatenate([wide_meta, upper_meta], axis=1), probe_modes, piece, rows, cols
    )
    piece = scatter_sum(gate(piece, upper_side, lower_side, scale), "x")
    piece = all_sum(piece, "z")
    mine = mine - piece[:4] / jnp.sqrt(piece[4:5] + 1.0)
    strip = collected(mine, "x")
    first_side = shifted(gate(first_side + below[:, :, cols:], strip), COL, 1)
    strip = jnp.roll(strip[::-1], x + 1, axis=0)
    whole = collected(strip, "y")
    whole = gate(whole, first_side)
    new_probe = run_join(jnp.stack([y, core]), whole, swapped(whole))
    new_object = run_finish(
        object_field, left_own, upper_own, lower_own, first_side, upper_side, lower_side, below, scale
    )
    return (new_object, new_probe.reshape(probe_modes.shape))


def solution(mesh):
    grid = Mesh(mesh.devices.reshape(4, 2, 4, 4), ROW + COL)
    placed = (
        P(None, ROW, COL),
        P(),
        P(ROW + COL, None, None),
        P(None, ROW + COL),
        P(ROW + COL),
    )
    return jax.shard_map(
        on_device,
        mesh=grid,
        in_specs=placed,
        out_specs=(P(None, ROW, COL), P()),
        check_vma=False,
    )
```

```python
import functools
import math

import jax
import jax.numpy as jnp
import ml_dtypes
import numpy as np
from jax import lax
from jax.experimental import pallas as pl
from jax.experimental.pallas import tpu as pltpu
from jax.sharding import Mesh
from jax.sharding import PartitionSpec as P

M = 256
ROOM = 56 * 1024 * 1024


def dft_tables(length):
    indices = np.arange(length)
    angles = (indices[:, None] * indices[None, :] % length) * (2.0 * math.pi / length)
    scale = 1.0 / math.sqrt(length)
    real = (np.cos(angles) * scale).astype(np.float32).astype(ml_dtypes.bfloat16)
    imag = (-np.sin(angles) * scale).astype(np.float32).astype(ml_dtypes.bfloat16)
    plain = np.block([[real, -imag], [imag, real]])
    conj = np.block([[real, imag], [-imag, real]])
    return plain, conj


def shifted(value, axis, steps):
    count = lax.axis_size(axis)
    first, last = (max(0, -steps), min(count, count - steps))
    return lax.ppermute(value, axis, [(source, source + steps) for source in range(first, last)])


def shifted_both(value, steps):
    rows, cols = lax.axis_size(ROW), lax.axis_size(COL)
    pairs = []
    for r in range(rows):
        for c in range(cols):
            if 0 <= r + steps < rows and 0 <= c + steps < cols:
                pairs.append((r * cols + c, (r + steps) * cols + c + steps))
    return lax.ppermute(value, ROW + COL, pairs)


def cut_strip(ref, channel, row_base, row_rest, col_base, col_rest, rows):
    lane = lax.broadcasted_iota(jnp.int32, (rows + 8, 128), 1)
    keep = lane < 128 - col_rest
    turn = (128 - col_rest) & 127
    tiles = [
        pltpu.roll(ref[channel, pl.ds(row_base, rows + 8), pl.ds(col_base + 128 * t, 128)], turn, 1)
        for t in range(3)
    ]
    groups = rows // 8
    sub = lax.broadcasted_iota(jnp.int32, (groups, 8, 128), 1)
    keep_rows = sub < 8 - row_rest
    turn_rows = (8 - row_rest) & 7
    out = []
    for t in range(2):
        joined = jnp.where(keep, tiles[t], tiles[t + 1]).reshape(groups + 1, 8, 128)
        turned = pltpu.roll(joined, turn_rows, 1)
        out.append(jnp.where(keep_rows, turned[:groups], turned[1:]).reshape(rows, 128))
    return jnp.concatenate(out, axis=1)


def add_strip(ref, channel, row_base, row_rest, col_base, col_rest, value):
    rows = value.shape[0]
    groups = rows // 8
    sub = lax.broadcasted_iota(jnp.int32, (groups, 8, 128), 1)
    keep_rows = sub >= row_rest
    lane = lax.broadcasted_iota(jnp.int32, (rows + 8, 128), 1)
    keep = lane >= col_rest
    halves = []
    for t in range(2):
        turned = pltpu.roll(value[:, 128 * t : 128 * (t + 1)].reshape(groups, 8, 128), row_rest, 1)
        upper = jnp.where(keep_rows, turned, 0.0)
        lower = turned - upper
        zero = jnp.zeros((1, 8, 128), jnp.float32)
        full = jnp.concatenate([upper, zero], 0) + jnp.concatenate([zero, lower], 0)
        halves.append(pltpu.roll(full.reshape(rows + 8, 128), col_rest, 1))
    zero = jnp.zeros_like(halves[0])
    parts = [
        jnp.where(keep, halves[0], zero),
        jnp.where(keep, halves[1], halves[0]),
        jnp.where(keep, zero, halves[1]),
    ]
    for t in range(3):
        at = (channel, pl.ds(row_base, rows + 8), pl.ds(col_base + 128 * t, 128))
        ref[at] = ref[at] + parts[t]


def split_at(index, step):
    base = (index // step) * step
    return pl.multiple_of(base, step), index - base


STRIP = 64
PIECE = 16


def wave_kernel(plan, meta, core, measured, probe, plain, conj, *refs):
    loads, inits, outs = plan["loads"], plan["inits"], plan["outs"]
    row_at, col_at, height, width = plan["region"]
    refs = list(refs)

    def take(count):
        taken, refs[:] = refs[:count], refs[count:]
        return taken

    load_refs, init_refs = take(len(loads)), take(len(inits))
    before = take(1)[0] if plan["follows"] else None
    passed = take(plan["passed"])
    take(plan["after"])
    out_refs = take(len(outs))
    sum_refs = take(2 if plan["last"] else 1)
    order, ext, acc, meas, sums, patch, wave, half, far, in_sem, meas_sem, out_sem = refs
    slots = meta.shape[1]

    copies = []

    def copy_in(source, target):
        copy = pltpu.make_async_copy(source, target, in_sem.at[len(copies)])
        copies.append(copy)
        copy.start()

    for (r, c, top, start, h, w), ref in zip(loads, load_refs):
        copy_in(ref.at[:, top : top + h, start : start + w], ext.at[:, r : r + h, c : c + w])

    if before is not None:
        copy_in(before, sums)
    for (r, c), ref in zip(inits, init_refs):
        copy_in(ref, acc.at[:, r : r + ref.shape[1], c : c + ref.shape[2]])

    def fetch(slot):
        return pltpu.make_async_copy(measured.at[slot], meas.at[slot], meas_sem.at[slot])

    count = jnp.int32(0)
    for slot in range(slots):
        row, col, live = meta[0, slot], meta[1, slot], meta[2, slot]
        mine = (live > 0) & (row >= plan["rows"][0]) & (row < plan["rows"][1])
        mine = mine & (col >= plan["cols"][0]) & (col < plan["cols"][1])

        @pl.when(mine)
        def _(slot=slot, count=count):
            order[count] = slot
            fetch(slot).start()

        count = count + mine.astype(jnp.int32)

    for r, c, h, w in plan["clear"]:

        def clear(at, carry, r=r, c=c, w=w):
            rows = pl.ds(pl.multiple_of(r + at * 32, 32), 32)
            acc[:, rows, c : c + w] = jnp.zeros((2, 32, w), jnp.float32)
            return carry

        lax.fori_loop(0, h // 32, clear, 0)
    if before is None:
        sums[...] = jnp.zeros_like(sums)
    for copy in copies:
        copy.wait()

    def left(use, table):
        for k in range(2):
            both = jnp.dot(table[...], wave[use, :, M * k : M * (k + 1)], preferred_element_type=jnp.float32)
            half[use, M * k : M * (k + 1), :M] = both[:M].astype(jnp.bfloat16)
            half[use, M * k : M * (k + 1), M:] = both[M:].astype(jnp.bfloat16)

    def right_mul(use, table):
        for part in range(2):
            far[use, :, M * part : M * (part + 1)] = jnp.dot(
                half[use], table[:, M * part : M * (part + 1)], preferred_element_type=jnp.float32
            )

    def add_sum(channel, at, value):
        for row in range(0, STRIP, PIECE):
            block = (at + row) // PIECE
            sums[0, block, channel] += value[row : row + PIECE, :128]
            sums[1, block, channel] += value[row : row + PIECE, 128:]

    def where(step):
        slot = order[step]
        row_base, row_rest = split_at(meta[0, slot] - row_at, 8)
        col_base, col_rest = split_at(meta[1, slot] - col_at, 128)
        return slot, row_base, row_rest, col_base, col_rest

    def cut(use, slot, row_base, row_rest, col_base, col_rest):
        for at in range(0, M, STRIP):
            rows = pl.ds(at, STRIP)
            base = pl.multiple_of(row_base + at, 8)
            o_re = cut_strip(ext, 0, base, row_rest, col_base, col_rest, STRIP)
            o_im = cut_strip(ext, 1, base, row_rest, col_base, col_rest, STRIP)
            patch[use, 0, rows, :] = o_re
            patch[use, 1, rows, :] = o_im
            add_sum(4, at, o_re * o_re + o_im * o_im)
            for k in range(2):
                p_re = probe[0, k, rows, :]
                p_im = probe[1, k, rows, :]
                cols = pl.ds(M * k, M)
                wave[use, rows, cols] = (p_re * o_re - p_im * o_im).astype(jnp.bfloat16)
                wave[use, pl.ds(M + at, STRIP), cols] = (p_re * o_im + p_im * o_re).astype(jnp.bfloat16)

    def resid(use, slot):
        fetch(slot).wait()
        for at in range(0, M, STRIP):
            rows = pl.ds(at, STRIP)
            parts = [
                [far[use, pl.ds(M * k + at, STRIP), M * part : M * (part + 1)] for part in range(2)]
                for k in range(2)
            ]
            intensity = parts[0][0] * parts[0][0] + parts[0][1] * parts[0][1]
            intensity = intensity + parts[1][0] * parts[1][0] + parts[1][1] * parts[1][1]
            level = meas[slot, rows, :]
            factor = 1.0 - level * lax.rsqrt(level * jnp.maximum(intensity, 0.25))
            for k in range(2):
                for part in range(2):
                    wave[use, pl.ds(M * part + at, STRIP), M * k : M * (k + 1)] = (
                        parts[k][part] * factor
                    ).astype(jnp.bfloat16)

    def grad(use, slot, row_base, row_rest, col_base, col_rest):
        for at in range(0, M, STRIP):
            rows = pl.ds(at, STRIP)
            base = pl.multiple_of(row_base + at, 8)
            o_re = patch[use, 0, rows, :]
            o_im = patch[use, 1, rows, :]
            g_re = None
            for k in range(2):
                n_re = far[use, pl.ds(M * k + at, STRIP), :M]
                n_im = far[use, pl.ds(M * k + at, STRIP), M:]
                p_re = probe[0, k, rows, :]
                p_im = probe[1, k, rows, :]
                add_sum(k, at, o_re * n_re + o_im * n_im)
                add_sum(2 + k, at, o_re * n_im - o_im * n_re)
                t_re = p_re * n_re + p_im * n_im
                t_im = p_re * n_im - p_im * n_re
                g_re, g_im = (t_re, t_im) if g_re is None else (g_re + t_re, g_im + t_im)
            add_strip(acc, 0, base, row_rest, col_base, col_rest, g_re)
            add_strip(acc, 1, base, row_rest, col_base, col_rest, g_im)

    def stages(use, step):
        at = where(step)
        return (
            lambda: cut(use, *at),
            lambda: left(use, plain),
            lambda: right_mul(use, conj),
            lambda: resid(use, at[0]),
            lambda: left(use, conj),
            lambda: right_mul(use, plain),
            lambda: grad(use, *at),
        )

    def visit_pair(pair, carry):
        first, second = stages(0, 2 * pair), stages(1, 2 * pair + 1)
        first[0]()
        for ahead, behind in zip(first[1:], second[:-1]):
            ahead()
            behind()
        second[-1]()
        return carry

    lax.fori_loop(0, count // 2, visit_pair, 0)

    @pl.when(count % 2 == 1)
    def _():
        for stage in stages(0, count - 1):
            stage()

    stores = []
    if plan["last"]:
        stores.append((sums.at[core[0]], sum_refs[0]))
        stores.append((sums.at[1 - core[0]], sum_refs[1]))
    else:
        stores.append((sums, sum_refs[0]))
    for (r, c, h, w, _), ref in zip(outs, out_refs):
        stores.append((acc.at[:, r : r + h, c : c + w], ref.at[:, :, ref.shape[2] - w :]))
    for ref in passed:
        stores.append((ref, out_refs[-1].at[:, :, : ref.shape[2]]))
    stores = [pltpu.make_async_copy(a, b, out_sem.at[i]) for i, (a, b) in enumerate(stores)]
    for copy in stores:
        copy.start()
    for copy in stores:
        copy.wait()


def run_waves(plan, meta, core, measured, probe, tables, loads, inits, before=None, passed=(), after=()):
    slots = measured.shape[0]
    height, width = plan["region"][2:]
    f32 = jnp.float32
    plan = dict(
        plan,
        loads=[place for place, _ in loads],
        inits=[place for place, _ in inits],
        follows=before is not None,
        passed=len(passed),
        after=len(after),
    )
    anywhere = pl.BlockSpec(memory_space=pl.ANY)
    vmem = pl.BlockSpec(memory_space=pltpu.VMEM)
    smem = pl.BlockSpec(memory_space=pltpu.SMEM)
    arrays = [array for _, array in loads] + [array for _, array in inits]
    arrays = arrays + ([] if before is None else [before]) + list(passed) + list(after)
    in_hbm = pl.BlockSpec(memory_space=pltpu.HBM)
    array_specs = [in_hbm if array is loads[0][1] else anywhere for array in arrays]
    shapes = [jax.ShapeDtypeStruct((2, h, w), f32) for _, _, h, w, _ in plan["outs"]]
    out_specs = [in_hbm if stays else anywhere for *_, stays in plan["outs"]]
    for array in passed:
        shapes[-1] = jax.ShapeDtypeStruct((2, M, array.shape[2] + shapes[-1].shape[2]), f32)
    if plan["last"]:
        shapes = shapes + [jax.ShapeDtypeStruct((M // PIECE, 5, PIECE, M // 2), f32)] * 2
    else:
        shapes = shapes + [jax.ShapeDtypeStruct((2, M // PIECE, 5, PIECE, M // 2), f32)]
    return pl.pallas_call(
        functools.partial(wave_kernel, plan),
        out_shape=shapes,
        in_specs=[smem, smem, in_hbm] + [vmem] * 3 + array_specs,
        out_specs=out_specs + [anywhere] * (len(shapes) - len(out_specs)),
        scratch_shapes=[
            pltpu.SMEM((slots,), jnp.int32),
            pltpu.VMEM((2, height, width), f32),
            pltpu.VMEM((2, height, width), f32),
            pltpu.VMEM((slots, M, M), f32),
            pltpu.VMEM((2, M // PIECE, 5, PIECE, M // 2), f32),
            pltpu.VMEM((2, 2, M, M), f32),
            pltpu.VMEM((2, 2 * M, 2 * M), jnp.bfloat16),
            pltpu.VMEM((2, 2 * M, 2 * M), jnp.bfloat16),
            pltpu.VMEM((2, 2 * M, 2 * M), f32),
            pltpu.SemaphoreType.DMA((len(arrays) + 1,)),
            pltpu.SemaphoreType.DMA((slots,)),
            pltpu.SemaphoreType.DMA((len(shapes) + 1,)),
        ],
        compiler_params=pltpu.CompilerParams(vmem_limit_bytes=34 * 1024 * 1024),
        cost_estimate=pl.CostEstimate(
            flops=10**8, bytes_accessed=2**20, transcendentals=0
        ),
        name=plan["name"],
    )(meta, core, measured, probe, *tables, *arrays)


def light_kernel(meta, probe, after, scale, light):
    slots = meta.shape[1]
    rows, cols = scale.shape
    light[...] = jnp.zeros_like(light)

    def visit(slot, carry):
        row, col = meta[0, slot], meta[1, slot]
        seen = (meta[2, slot] > 0) & (row > -M) & (row < rows) & (col > -M) & (col < cols)

        @pl.when(seen)
        def _():
            row_base, row_rest = split_at(row + M, 8)
            col_base, col_rest = split_at(col + M, 128)
            for at in range(0, M, STRIP):
                here = pl.ds(at, STRIP)
                value = probe[0, 0, here, :] * probe[0, 0, here, :]
                for part, k in ((1, 0), (0, 1), (1, 1)):
                    value = value + probe[part, k, here, :] * probe[part, k, here, :]
                base = pl.multiple_of(row_base + at, 8)
                add_strip(light, 0, base, row_rest, col_base, col_rest, value)

        return carry

    lax.fori_loop(0, slots, visit, 0)
    for at in range(0, rows, 64):
        scale[at : at + 64, :] = lax.rsqrt(light[0, M + at : M + at + 64, M : M + cols] + 1.0)


def run_light(meta, probe, after, rows, cols):
    return pl.pallas_call(
        light_kernel,
        out_shape=jax.ShapeDtypeStruct((rows, cols), jnp.float32),
        in_specs=[
            pl.BlockSpec(memory_space=pltpu.SMEM),
            pl.BlockSpec(memory_space=pltpu.VMEM),
            pl.BlockSpec(memory_space=pl.ANY),
        ],
        out_specs=pl.BlockSpec(memory_space=pltpu.VMEM),
        scratch_shapes=[pltpu.VMEM((1, rows + 2 * M, cols + 2 * M), jnp.float32)],
        compiler_params=pltpu.CompilerParams(vmem_limit_bytes=20 * 1024 * 1024),
        cost_estimate=pl.CostEstimate(flops=10**8, bytes_accessed=24 * 2**20, transcendentals=0),
        name="light",
    )(meta, probe, after)


def finish_kernel(
    tile, left_own, upper_own, lower_own, first_side, upper_side, lower_side, below, scale, out
):
    step = pl.program_id(0)
    factor = scale[...][None]

    def write(own, side):
        out[:, :, :M] = tile[:, :, :M] - (left_own[...] + side[...]) * factor[:, :, :M]
        out[:, :, M:] = tile[:, :, M:] - own[...] * factor[:, :, M:]

    @pl.when(step == 0)
    def _():
        write(upper_own, first_side)
        out[...] = out[...] - below[...] * factor

    @pl.when(step == 1)
    def _():
        write(upper_own, upper_side)

    @pl.when(step > 1)
    def _():
        write(lower_own, lower_side)


def run_finish(tile, left_own, upper_own, lower_own, first_side, upper_side, lower_side, below, scale):
    rows, cols = tile.shape[1], tile.shape[2]
    steps = rows // M
    half = steps // 2
    block = pl.BlockSpec((2, M, cols), lambda i: (0, i, 0))
    upper = pl.BlockSpec((2, M, M), lambda i: (0, jnp.minimum(i, half - 1), 0))
    lower = pl.BlockSpec((2, M, M), lambda i: (0, jnp.maximum(i - half, 0), 0))
    first = pl.BlockSpec((2, M, M), lambda i: (0, 0, 0))
    return pl.pallas_call(
        finish_kernel,
        grid=(steps,),
        out_shape=jax.ShapeDtypeStruct(tile.shape, jnp.float32),
        in_specs=[
            block,
            pl.BlockSpec((2, M, M), lambda i: (0, i, 0)),
            upper,
            lower,
            first,
            first,
            lower,
            pl.BlockSpec((2, M, cols), lambda i: (0, 0, 0)),
            pl.BlockSpec((M, cols), lambda i: (i, 0)),
        ],
        out_specs=block,
        compiler_params=pltpu.CompilerParams(vmem_limit_bytes=ROOM),
        cost_estimate=pl.CostEstimate(flops=10**7, bytes_accessed=20 * 2**20, transcendentals=0),
        name="finish",
    )(tile, left_own, upper_own, lower_own, first_side, upper_side, lower_side, below, scale)


def cut_kernel(pieces, after, tile, *refs):
    outs, sem = refs[after:-1], refs[-1]
    copies = [
        pltpu.make_async_copy(tile.at[:, r : r + h, :w], out, sem.at[i])
        for i, ((r, h, w), out) in enumerate(zip(pieces, outs))
    ]
    for copy in copies:
        copy.start()
    for copy in copies:
        copy.wait()


def run_cut(tile, pieces, *after):
    anywhere = pl.BlockSpec(memory_space=pl.ANY)
    return pl.pallas_call(
        functools.partial(cut_kernel, pieces, len(after)),
        out_shape=[jax.ShapeDtypeStruct((2, h, w), jnp.float32) for _, h, w in pieces],
        in_specs=[anywhere] * (1 + len(after)),
        out_specs=[pl.BlockSpec(memory_space=pltpu.VMEM)] * len(pieces),
        scratch_shapes=[pltpu.SemaphoreType.DMA((len(pieces),))],
        compiler_params=pltpu.CompilerParams(vmem_limit_bytes=ROOM),
        name="cut",
    )(tile, *after)


def join_kernel(place, mine, other, out):
    y = place[0]
    first = place[1] == 0
    for back in range(mine.shape[0]):
        for x in range(mine.shape[1]):
            row = ((y - back) & 3) * (M // 4) + x * PIECE
            rows = pl.ds(pl.multiple_of(row, PIECE), PIECE)
            for channel in range(4):
                a, b = mine[back, x, channel], other[back, x, channel]
                out[channel, rows, : M // 2] = jnp.where(first, a, b)
                out[channel, rows, M // 2 :] = jnp.where(first, b, a)


def run_join(place, mine, other):
    vmem = pl.BlockSpec(memory_space=pltpu.VMEM)
    return pl.pallas_call(
        join_kernel,
        out_shape=jax.ShapeDtypeStruct((4, M, M), jnp.float32),
        in_specs=[pl.BlockSpec(memory_space=pltpu.SMEM), vmem, vmem],
        out_specs=vmem,
        compiler_params=pltpu.CompilerParams(vmem_limit_bytes=8 * 1024 * 1024),
        name="join",
    )(place, mine, other)


def nothing(value, *rest):
    pass


def gate(value, *after):
    anywhere = pl.BlockSpec(memory_space=pl.ANY)
    return pl.pallas_call(
        nothing,
        out_shape=jax.ShapeDtypeStruct(value.shape, value.dtype),
        in_specs=[anywhere] * (1 + len(after)),
        out_specs=anywhere,
        input_output_aliases={0: 0},
        compiler_params=pltpu.CompilerParams(vmem_limit_bytes=2**20),
        name="gate",
    )(value, *after)


ROW, COL = ("y", "core"), ("x", "z")


def turned(value, axis, steps):
    count = lax.axis_size(axis)
    return lax.ppermute(value, axis, [(at, (at + steps) % count) for at in range(count)])


def swapped(value):
    return turned(value, "core", 1)


def scatter_sum(value, axis):
    count, me = lax.axis_size(axis), lax.axis_index(axis)
    parts = [
        lax.dynamic_index_in_dim(value, (me + steps) % count, 0, keepdims=False)
        for steps in range(count)
    ]
    others = [turned(parts[steps], axis, steps) for steps in range(1, count)]
    return functools.reduce(jnp.add, others, parts[0])


def all_sum(value, axis):
    others = [turned(value, axis, steps) for steps in range(1, lax.axis_size(axis))]
    return functools.reduce(jnp.add, others, value)


def collected(value, axis):
    others = [turned(value, axis, steps) for steps in range(1, lax.axis_size(axis))]
    return jnp.stack([value] + others)


def on_device(object_field, probe_modes, measured, offsets, live_slots):
    rows, cols = object_field.shape[1], object_field.shape[2]
    tables = tuple(jnp.asarray(table) for table in dft_tables(M))
    mid = rows // 2
    meta = jnp.concatenate(
        [
            offsets[0:1] - lax.axis_index(ROW) * rows,
            offsets[1:2] - lax.axis_index(COL) * cols,
            live_slots[None],
        ],
        axis=0,
    )
    first_cols, top_rows = run_cut(object_field, ((0, mid + M, M), (0, M, cols)))
    left_meta = shifted(meta, COL, 1) - jnp.array([[0], [cols], [0]], jnp.int32)
    wide_meta = jnp.concatenate([meta, left_meta], axis=1)
    upper_meta = shifted(wide_meta, ROW, 1) - jnp.array([[rows], [0], [0]], jnp.int32)
    (last_cols,) = run_cut(object_field, ((mid + M, M, M),), left_meta)
    first_cols = shifted(first_cols, COL, -1)
    last_cols = shifted(last_cols, COL, -1)
    lower = shifted(top_rows, ROW, -1)
    core, y, x = (lax.axis_index(axis) for axis in ("core", "y", "x"))
    mine = lax.dynamic_slice(
        probe_modes.reshape(4, M, M),
        (0, y * (M // 4) + x * PIECE, core * (M // 2)),
        (4, PIECE, M // 2),
    )
    common = (meta, core[None], measured, probe_modes, tables)

    plan = dict(
        name="left",
        region=(0, 0, rows + M, cols),
        rows=(0, rows),
        cols=(0, M),
        clear=[(0, 0, rows + M, cols)],
        outs=[
            (0, 0, rows, M, True),
            (0, M, mid + M, M, False),
            (mid + M, M, mid, M, False),
            (rows, 0, M, M, False),
        ],
        last=False,
    )
    left_own, upper_init, lower_init, below_left, sums = run_waves(
        plan,
        *common,
        [((0, 0, 0, 0, rows, cols), object_field), ((rows, 0, 0, 0, M, cols), lower)],
        [],
        after=(upper_meta,),
    )
    corner = shifted(gate(first_cols[:, :M], sums), ROW, -1)
    plan = dict(
        name="upper",
        region=(0, M, mid + M, cols),
        rows=(0, mid),
        cols=(M, cols),
        clear=[(0, M, mid + M, M)],
        outs=[
            (0, 0, mid, M, True),
            (0, M, M, M, False),
            (M, M, M, M, False),
            (mid, 0, M, cols, False),
        ],
        last=False,
    )
    upper_own, first_side, upper_side, middle, sums = run_waves(
        plan,
        *common,
        [
            ((0, 0, 0, M, mid + M, M), object_field),
            ((0, M, 0, 0, mid + M, M), first_cols),
        ],
        [((0, 0), upper_init)],
        before=sums,
    )
    plan = dict(
        name="lower",
        region=(mid, M, mid + M, cols),
        rows=(mid, rows),
        cols=(M, cols),
        clear=[(M, M, mid, M)],
        outs=[(0, 0, mid, M, True), (0, M, mid, M, False), (mid, 0, M, cols, False)],
        last=True,
    )
    lower_own, lower_side, below, kept, sent = run_waves(
        plan,
        *common,
        [
            ((0, 0, mid, M, mid, M), object_field),
            ((0, M, mid, 0, M, M), first_cols),
            ((M, M, 0, 0, M, M), last_cols),
            ((mid, 0, 0, M, M, M), lower),
            ((mid, M, 0, 0, M, M), corner),
        ],
        [((0, 0), middle), ((M, 0), lower_init)],
        before=sums,
        passed=(below_left,),
    )
    upper_side = shifted(upper_side, COL, 1)
    lower_side = shifted(lower_side, COL, 1)
    total = (kept + swapped(gate(sent, upper_side))).reshape(4, 4, 5, PIECE, M // 2)
    piece = scatter_sum(total, "y")
    below = shifted(gate(below, piece), ROW, 1)
    scale = run_light(
        jnp.concatenate([wide_meta, upper_meta], axis=1), probe_modes, piece, rows, cols
    )
    piece = scatter_sum(gate(piece, upper_side, lower_side, scale), "x")
    piece = all_sum(piece, "z")
    mine = mine - piece[:4] / jnp.sqrt(piece[4:5] + 1.0)
    strip = collected(mine, "x")
    first_side = shifted(gate(first_side + below[:, :, cols:], strip), COL, 1)
    strip = jnp.roll(strip[::-1], x + 1, axis=0)
    whole = collected(strip, "y")
    whole = gate(whole, first_side)
    new_probe = run_join(jnp.stack([y, core]), whole, swapped(whole))
    new_object = run_finish(
        object_field, left_own, upper_own, lower_own, first_side, upper_side, lower_side, below, scale
    )
    return (new_object, new_probe.reshape(probe_modes.shape))


def solution(mesh):
    grid = Mesh(mesh.devices.reshape(4, 2, 4, 4), ROW + COL)
    placed = (
        P(None, ROW, COL),
        P(),
        P(ROW + COL, None, None),
        P(None, ROW + COL),
        P(ROW + COL),
    )
    return jax.shard_map(
        on_device,
        mesh=grid,
        in_specs=placed,
        out_specs=(P(None, ROW, COL), P()),
        check_vma=False,
    )
```

```python
import functools
import math

import jax
import jax.numpy as jnp
import ml_dtypes
import numpy as np
from jax import lax
from jax.experimental import pallas as pl
from jax.experimental.pallas import tpu as pltpu
from jax.sharding import Mesh
from jax.sharding import PartitionSpec as P

M = 256
H = M // 2
ROOM = 56 * 1024 * 1024


def dft_tables(length):
    indices = np.arange(length)
    angles = (indices[:, None] * indices[None, :] % length) * (2.0 * math.pi / length)
    scale = 1.0 / math.sqrt(length)
    real = (np.cos(angles) * scale).astype(np.float32).astype(ml_dtypes.bfloat16)
    imag = (-np.sin(angles) * scale).astype(np.float32).astype(ml_dtypes.bfloat16)
    plain = np.block([[real, -imag], [imag, real]])
    conj = np.block([[real, imag], [-imag, real]])
    half = length // 2
    order = np.concatenate([np.arange(0, length, 2), np.arange(1, length, 2)])
    ahead = plain[np.concatenate([order, length + order])]
    back = []
    for first in range(2):
        re, im = real[:half, first::2], imag[:half, first::2]
        back.append(np.block([[re, im], [-im, re]]))
    return plain, conj, ahead, np.stack(back)


def shifted(value, axis, steps):
    count = lax.axis_size(axis)
    first, last = (max(0, -steps), min(count, count - steps))
    return lax.ppermute(value, axis, [(source, source + steps) for source in range(first, last)])


def shifted_both(value, steps):
    rows, cols = lax.axis_size(ROW), lax.axis_size(COL)
    pairs = []
    for r in range(rows):
        for c in range(cols):
            if 0 <= r + steps < rows and 0 <= c + steps < cols:
                pairs.append((r * cols + c, (r + steps) * cols + c + steps))
    return lax.ppermute(value, ROW + COL, pairs)


def cut_strip(ref, channel, row_base, row_rest, col_base, col_rest, rows):
    lane = lax.broadcasted_iota(jnp.int32, (rows + 8, 128), 1)
    keep = lane < 128 - col_rest
    turn = (128 - col_rest) & 127
    tiles = [
        pltpu.roll(ref[channel, pl.ds(row_base, rows + 8), pl.ds(col_base + 128 * t, 128)], turn, 1)
        for t in range(3)
    ]
    groups = rows // 8
    sub = lax.broadcasted_iota(jnp.int32, (groups, 8, 128), 1)
    keep_rows = sub < 8 - row_rest
    turn_rows = (8 - row_rest) & 7
    out = []
    for t in range(2):
        joined = jnp.where(keep, tiles[t], tiles[t + 1]).reshape(groups + 1, 8, 128)
        turned = pltpu.roll(joined, turn_rows, 1)
        out.append(jnp.where(keep_rows, turned[:groups], turned[1:]).reshape(rows, 128))
    return jnp.concatenate(out, axis=1)


def add_strip(ref, channel, row_base, row_rest, col_base, col_rest, value):
    rows = value.shape[0]
    groups = rows // 8
    sub = lax.broadcasted_iota(jnp.int32, (groups, 8, 128), 1)
    keep_rows = sub >= row_rest
    lane = lax.broadcasted_iota(jnp.int32, (rows + 8, 128), 1)
    keep = lane >= col_rest
    halves = []
    for t in range(2):
        turned = pltpu.roll(value[:, 128 * t : 128 * (t + 1)].reshape(groups, 8, 128), row_rest, 1)
        upper = jnp.where(keep_rows, turned, 0.0)
        lower = turned - upper
        zero = jnp.zeros((1, 8, 128), jnp.float32)
        full = jnp.concatenate([upper, zero], 0) + jnp.concatenate([zero, lower], 0)
        halves.append(pltpu.roll(full.reshape(rows + 8, 128), col_rest, 1))
    zero = jnp.zeros_like(halves[0])
    parts = [
        jnp.where(keep, halves[0], zero),
        jnp.where(keep, halves[1], halves[0]),
        jnp.where(keep, zero, halves[1]),
    ]
    for t in range(3):
        at = (channel, pl.ds(row_base, rows + 8), pl.ds(col_base + 128 * t, 128))
        ref[at] = ref[at] + parts[t]


def split_at(index, step):
    base = (index // step) * step
    return pl.multiple_of(base, step), index - base


STRIP = 64
PIECE = 16


def wave_kernel(plan, meta, core, measured, probe, plain, conj, split, back, *refs):
    loads, inits, outs = plan["loads"], plan["inits"], plan["outs"]
    row_at, col_at, height, width = plan["region"]
    refs = list(refs)

    def take(count):
        taken, refs[:] = refs[:count], refs[count:]
        return taken

    load_refs, init_refs = take(len(loads)), take(len(inits))
    before = take(1)[0] if plan["follows"] else None
    passed = take(plan["passed"])
    take(plan["after"])
    out_refs = take(len(outs))
    sum_refs = take(2 if plan["last"] else 1)
    order, ext, acc, meas, sums, patch, wave, half, far, in_sem, meas_sem, out_sem = refs
    slots = meta.shape[1]

    copies = []

    def copy_in(source, target):
        copy = pltpu.make_async_copy(source, target, in_sem.at[len(copies)])
        copies.append(copy)
        copy.start()

    for (r, c, top, start, h, w), ref in zip(loads, load_refs):
        copy_in(ref.at[:, top : top + h, start : start + w], ext.at[:, r : r + h, c : c + w])

    handed = [
        pltpu.make_async_copy(
            ref, out_refs[-1].at[:, :, : ref.shape[2]], out_sem.at[len(out_refs) + len(sum_refs) + at]
        )
        for at, ref in enumerate(passed)
    ]
    for copy in handed:
        copy.start()
    if before is not None:
        copy_in(before, sums)
    for (r, c), ref in zip(inits, init_refs):
        copy_in(ref, acc.at[:, r : r + ref.shape[1], c : c + ref.shape[2]])

    def fetch(slot):
        return [
            pltpu.make_async_copy(
                measured.at[slot, :, H * side : H * (side + 1)], meas.at[slot, side], meas_sem.at[slot, side]
            )
            for side in range(2)
        ]

    count = jnp.int32(0)
    for slot in range(slots):
        row, col, live = meta[0, slot], meta[1, slot], meta[2, slot]
        mine = (live > 0) & (row >= plan["rows"][0]) & (row < plan["rows"][1])
        mine = mine & (col >= plan["cols"][0]) & (col < plan["cols"][1])

        @pl.when(mine)
        def _(slot=slot, count=count):
            order[count] = slot
            for copy in fetch(slot):
                copy.start()

        count = count + mine.astype(jnp.int32)

    for r, c, h, w in plan["clear"]:

        def clear(at, carry, r=r, c=c, w=w):
            rows = pl.ds(pl.multiple_of(r + at * 32, 32), 32)
            acc[:, rows, c : c + w] = jnp.zeros((2, 32, w), jnp.float32)
            return carry

        lax.fori_loop(0, h // 32, clear, 0)
    if before is None:
        sums[...] = jnp.zeros_like(sums)
    for copy in copies:
        copy.wait()

    def left(use, table):
        for k in range(2):
            both = jnp.dot(table[...], wave[use, :, M * k : M * (k + 1)], preferred_element_type=jnp.float32)
            half[use, M * k : M * (k + 1), :M] = both[:M].astype(jnp.bfloat16)
            half[use, M * k : M * (k + 1), M:] = both[M:].astype(jnp.bfloat16)

    def left_back(use):
        for k in range(2):
            even, odd = (
                jnp.dot(
                    back[at],
                    wave[use, M * at : M * (at + 1), M * k : M * (k + 1)],
                    preferred_element_type=jnp.float32,
                )
                for at in range(2)
            )
            for side, both in enumerate((even + odd, even - odd)):
                for part in range(2):
                    half[use, M * k + H * side : M * k + H * (side + 1), M * part : M * (part + 1)] = both[
                        H * part : H * (part + 1)
                    ].astype(jnp.bfloat16)

    def right_mul(use, table):
        for part in range(2):
            far[use, :, M * part : M * (part + 1)] = jnp.dot(
                half[use], table[:, M * part : M * (part + 1)], preferred_element_type=jnp.float32
            )

    def add_sum(channel, at, value):
        for row in range(0, STRIP, PIECE):
            block = (at + row) // PIECE
            sums[0, block, channel] += value[row : row + PIECE, :128]
            sums[1, block, channel] += value[row : row + PIECE, 128:]

    def where(step):
        slot = order[step]
        row_base, row_rest = split_at(meta[0, slot] - row_at, 8)
        col_base, col_rest = split_at(meta[1, slot] - col_at, 128)
        return slot, row_base, row_rest, col_base, col_rest

    def cut(use, slot, row_base, row_rest, col_base, col_rest):
        for at in range(0, M, STRIP):
            rows = pl.ds(at, STRIP)
            base = pl.multiple_of(row_base + at, 8)
            o_re = cut_strip(ext, 0, base, row_rest, col_base, col_rest, STRIP)
            o_im = cut_strip(ext, 1, base, row_rest, col_base, col_rest, STRIP)
            patch[use, 0, rows, :] = o_re
            patch[use, 1, rows, :] = o_im
            add_sum(4, at, o_re * o_re + o_im * o_im)
            for k in range(2):
                p_re = probe[0, k, rows, :]
                p_im = probe[1, k, rows, :]
                cols = pl.ds(M * k, M)
                wave[use, rows, cols] = (p_re * o_re - p_im * o_im).astype(jnp.bfloat16)
                wave[use, pl.ds(M + at, STRIP), cols] = (p_re * o_im + p_im * o_re).astype(jnp.bfloat16)

    def resid(use, slot):
        for copy in fetch(slot):
            copy.wait()
        for at in range(0, M, STRIP):
            odd, start = at // H, at % H
            parts = [
                [far[use, pl.ds(M * k + at, STRIP), M * part : M * (part + 1)] for part in range(2)]
                for k in range(2)
            ]
            intensity = parts[0][0] * parts[0][0] + parts[0][1] * parts[0][1]
            intensity = intensity + parts[1][0] * parts[1][0] + parts[1][1] * parts[1][1]
            level = jnp.concatenate(
                [meas[slot, side, pl.ds(2 * start + odd, STRIP, 2), :] for side in range(2)], axis=1
            )
            factor = 1.0 - level * lax.rsqrt(level * jnp.maximum(intensity, 0.25))
            for k in range(2):
                for part in range(2):
                    wave[use, pl.ds(M * odd + H * part + start, STRIP), M * k : M * (k + 1)] = (
                        parts[k][part] * factor
                    ).astype(jnp.bfloat16)

    def grad(use, slot, row_base, row_rest, col_base, col_rest):
        for at in range(0, M, STRIP):
            rows = pl.ds(at, STRIP)
            base = pl.multiple_of(row_base + at, 8)
            o_re = patch[use, 0, rows, :]
            o_im = patch[use, 1, rows, :]
            g_re = None
            for k in range(2):
                n_re = far[use, pl.ds(M * k + at, STRIP), :M]
                n_im = far[use, pl.ds(M * k + at, STRIP), M:]
                p_re = probe[0, k, rows, :]
                p_im = probe[1, k, rows, :]
                add_sum(k, at, o_re * n_re + o_im * n_im)
                add_sum(2 + k, at, o_re * n_im - o_im * n_re)
                t_re = p_re * n_re + p_im * n_im
                t_im = p_re * n_im - p_im * n_re
                g_re, g_im = (t_re, t_im) if g_re is None else (g_re + t_re, g_im + t_im)
            add_strip(acc, 0, base, row_rest, col_base, col_rest, g_re)
            add_strip(acc, 1, base, row_rest, col_base, col_rest, g_im)

    def stages(use, step):
        at = where(step)
        return (
            lambda: cut(use, *at),
            lambda: left(use, split),
            lambda: right_mul(use, conj),
            lambda: resid(use, at[0]),
            lambda: left_back(use),
            lambda: right_mul(use, plain),
            lambda: grad(use, *at),
        )

    def visit_pair(pair, carry):
        first, second = stages(0, 2 * pair), stages(1, 2 * pair + 1)
        first[0]()
        for ahead, behind in zip(first[1:], second[:-1]):
            ahead()
            behind()
        second[-1]()
        return carry

    lax.fori_loop(0, count // 2, visit_pair, 0)

    @pl.when(count % 2 == 1)
    def _():
        for stage in stages(0, count - 1):
            stage()

    stores = []
    if plan["last"]:
        stores.append((sums.at[core[0]], sum_refs[0]))
        stores.append((sums.at[1 - core[0]], sum_refs[1]))
    else:
        stores.append((sums, sum_refs[0]))
    for (r, c, h, w, _), ref in zip(outs, out_refs):
        stores.append((acc.at[:, r : r + h, c : c + w], ref.at[:, :, ref.shape[2] - w :]))
    stores = [pltpu.make_async_copy(a, b, out_sem.at[i]) for i, (a, b) in enumerate(stores)]
    for copy in stores:
        copy.start()
    for copy in handed + stores:
        copy.wait()


def run_waves(plan, meta, core, measured, probe, tables, loads, inits, before=None, passed=(), after=()):
    slots = measured.shape[0]
    height, width = plan["region"][2:]
    f32 = jnp.float32
    plan = dict(
        plan,
        loads=[place for place, _ in loads],
        inits=[place for place, _ in inits],
        follows=before is not None,
        passed=len(passed),
        after=len(after),
    )
    anywhere = pl.BlockSpec(memory_space=pl.ANY)
    vmem = pl.BlockSpec(memory_space=pltpu.VMEM)
    smem = pl.BlockSpec(memory_space=pltpu.SMEM)
    arrays = [array for _, array in loads] + [array for _, array in inits]
    arrays = arrays + ([] if before is None else [before]) + list(passed) + list(after)
    in_hbm = pl.BlockSpec(memory_space=pltpu.HBM)
    array_specs = [in_hbm if array is loads[0][1] else anywhere for array in arrays]
    shapes = [jax.ShapeDtypeStruct((2, h, w), f32) for _, _, h, w, _ in plan["outs"]]
    out_specs = [in_hbm if stays else anywhere for *_, stays in plan["outs"]]
    for array in passed:
        shapes[-1] = jax.ShapeDtypeStruct((2, M, array.shape[2] + shapes[-1].shape[2]), f32)
    if plan["last"]:
        shapes = shapes + [jax.ShapeDtypeStruct((M // PIECE, 5, PIECE, M // 2), f32)] * 2
    else:
        shapes = shapes + [jax.ShapeDtypeStruct((2, M // PIECE, 5, PIECE, M // 2), f32)]
    return pl.pallas_call(
        functools.partial(wave_kernel, plan),
        out_shape=shapes,
        in_specs=[smem, smem, in_hbm] + [vmem] * 5 + array_specs,
        out_specs=out_specs + [anywhere] * (len(shapes) - len(out_specs)),
        scratch_shapes=[
            pltpu.SMEM((slots,), jnp.int32),
            pltpu.VMEM((2, height, width), f32),
            pltpu.VMEM((2, height, width), f32),
            pltpu.VMEM((slots, 2, M, H), f32),
            pltpu.VMEM((2, M // PIECE, 5, PIECE, M // 2), f32),
            pltpu.VMEM((2, 2, M, M), f32),
            pltpu.VMEM((2, 2 * M, 2 * M), jnp.bfloat16),
            pltpu.VMEM((2, 2 * M, 2 * M), jnp.bfloat16),
            pltpu.VMEM((2, 2 * M, 2 * M), f32),
            pltpu.SemaphoreType.DMA((len(arrays) + 1,)),
            pltpu.SemaphoreType.DMA((slots, 2)),
            pltpu.SemaphoreType.DMA((len(shapes) + 1,)),
        ],
        compiler_params=pltpu.CompilerParams(vmem_limit_bytes=34 * 1024 * 1024),
        cost_estimate=pl.CostEstimate(
            flops=10**8, bytes_accessed=2**20, transcendentals=0
        ),
        name=plan["name"],
    )(meta, core, measured, probe, *tables, *arrays)


def light_kernel(meta, probe, after, scale, light):
    slots = meta.shape[1]
    rows, cols = scale.shape
    light[...] = jnp.zeros_like(light)

    def visit(slot, carry):
        row, col = meta[0, slot], meta[1, slot]
        seen = (meta[2, slot] > 0) & (row > -M) & (row < rows) & (col > -M) & (col < cols)

        @pl.when(seen)
        def _():
            row_base, row_rest = split_at(row + M, 8)
            col_base, col_rest = split_at(col + M, 128)
            for at in range(0, M, STRIP):
                here = pl.ds(at, STRIP)
                value = probe[0, 0, here, :] * probe[0, 0, here, :]
                for part, k in ((1, 0), (0, 1), (1, 1)):
                    value = value + probe[part, k, here, :] * probe[part, k, here, :]
                base = pl.multiple_of(row_base + at, 8)
                add_strip(light, 0, base, row_rest, col_base, col_rest, value)

        return carry

    lax.fori_loop(0, slots, visit, 0)
    for at in range(0, rows, 64):
        scale[at : at + 64, :] = lax.rsqrt(light[0, M + at : M + at + 64, M : M + cols] + 1.0)


def run_light(meta, probe, after, rows, cols):
    return pl.pallas_call(
        light_kernel,
        out_shape=jax.ShapeDtypeStruct((rows, cols), jnp.float32),
        in_specs=[
            pl.BlockSpec(memory_space=pltpu.SMEM),
            pl.BlockSpec(memory_space=pltpu.VMEM),
            pl.BlockSpec(memory_space=pl.ANY),
        ],
        out_specs=pl.BlockSpec(memory_space=pltpu.VMEM),
        scratch_shapes=[pltpu.VMEM((1, rows + 2 * M, cols + 2 * M), jnp.float32)],
        compiler_params=pltpu.CompilerParams(vmem_limit_bytes=20 * 1024 * 1024),
        cost_estimate=pl.CostEstimate(flops=10**8, bytes_accessed=24 * 2**20, transcendentals=0),
        name="light",
    )(meta, probe, after)


def finish_kernel(
    tile, left_own, upper_own, lower_own, first_side, upper_side, lower_side, below, scale, out
):
    step = pl.program_id(0)
    factor = scale[...][None]

    def write(own, side):
        out[:, :, :M] = tile[:, :, :M] - (left_own[...] + side[...]) * factor[:, :, :M]
        out[:, :, M:] = tile[:, :, M:] - own[...] * factor[:, :, M:]

    @pl.when(step == 0)
    def _():
        write(upper_own, first_side)
        out[...] = out[...] - below[...] * factor

    @pl.when(step == 1)
    def _():
        write(upper_own, upper_side)

    @pl.when(step > 1)
    def _():
        write(lower_own, lower_side)


def run_finish(tile, left_own, upper_own, lower_own, first_side, upper_side, lower_side, below, scale):
    rows, cols = tile.shape[1], tile.shape[2]
    steps = rows // M
    half = steps // 2
    block = pl.BlockSpec((2, M, cols), lambda i: (0, i, 0))
    upper = pl.BlockSpec((2, M, M), lambda i: (0, jnp.minimum(i, half - 1), 0))
    lower = pl.BlockSpec((2, M, M), lambda i: (0, jnp.maximum(i - half, 0), 0))
    first = pl.BlockSpec((2, M, M), lambda i: (0, 0, 0))
    return pl.pallas_call(
        finish_kernel,
        grid=(steps,),
        out_shape=jax.ShapeDtypeStruct(tile.shape, jnp.float32),
        in_specs=[
            block,
            pl.BlockSpec((2, M, M), lambda i: (0, i, 0)),
            upper,
            lower,
            first,
            first,
            lower,
            pl.BlockSpec((2, M, cols), lambda i: (0, 0, 0)),
            pl.BlockSpec((M, cols), lambda i: (i, 0)),
        ],
        out_specs=block,
        compiler_params=pltpu.CompilerParams(vmem_limit_bytes=ROOM),
        cost_estimate=pl.CostEstimate(flops=10**7, bytes_accessed=20 * 2**20, transcendentals=0),
        name="finish",
    )(tile, left_own, upper_own, lower_own, first_side, upper_side, lower_side, below, scale)


def cut_kernel(pieces, after, tile, *refs):
    outs, sem = refs[after:-1], refs[-1]
    copies = [
        pltpu.make_async_copy(tile.at[:, r : r + h, :w], out, sem.at[i])
        for i, ((r, h, w), out) in enumerate(zip(pieces, outs))
    ]
    for copy in copies:
        copy.start()
    for copy in copies:
        copy.wait()


def run_cut(tile, pieces, *after):
    anywhere = pl.BlockSpec(memory_space=pl.ANY)
    return pl.pallas_call(
        functools.partial(cut_kernel, pieces, len(after)),
        out_shape=[jax.ShapeDtypeStruct((2, h, w), jnp.float32) for _, h, w in pieces],
        in_specs=[anywhere] * (1 + len(after)),
        out_specs=[pl.BlockSpec(memory_space=pltpu.VMEM)] * len(pieces),
        scratch_shapes=[pltpu.SemaphoreType.DMA((len(pieces),))],
        compiler_params=pltpu.CompilerParams(vmem_limit_bytes=ROOM),
        name="cut",
    )(tile, *after)


def join_kernel(place, mine, other, out):
    y = place[0]
    first = place[1] == 0
    for back in range(mine.shape[0]):
        for x in range(mine.shape[1]):
            row = ((y - back) & 3) * (M // 4) + x * PIECE
            rows = pl.ds(pl.multiple_of(row, PIECE), PIECE)
            for channel in range(4):
                a, b = mine[back, x, channel], other[back, x, channel]
                out[channel, rows, : M // 2] = jnp.where(first, a, b)
                out[channel, rows, M // 2 :] = jnp.where(first, b, a)


def run_join(place, mine, other):
    vmem = pl.BlockSpec(memory_space=pltpu.VMEM)
    return pl.pallas_call(
        join_kernel,
        out_shape=jax.ShapeDtypeStruct((4, M, M), jnp.float32),
        in_specs=[pl.BlockSpec(memory_space=pltpu.SMEM), vmem, vmem],
        out_specs=vmem,
        compiler_params=pltpu.CompilerParams(vmem_limit_bytes=8 * 1024 * 1024),
        name="join",
    )(place, mine, other)


def nothing(value, *rest):
    pass


def gate(value, *after):
    anywhere = pl.BlockSpec(memory_space=pl.ANY)
    return pl.pallas_call(
        nothing,
        out_shape=jax.ShapeDtypeStruct(value.shape, value.dtype),
        in_specs=[anywhere] * (1 + len(after)),
        out_specs=anywhere,
        input_output_aliases={0: 0},
        compiler_params=pltpu.CompilerParams(vmem_limit_bytes=2**20),
        name="gate",
    )(value, *after)


ROW, COL = ("y", "core"), ("x", "z")


def turned(value, axis, steps):
    count = lax.axis_size(axis)
    return lax.ppermute(value, axis, [(at, (at + steps) % count) for at in range(count)])


def swapped(value):
    return turned(value, "core", 1)


def scatter_sum(value, axis):
    count, me = lax.axis_size(axis), lax.axis_index(axis)
    parts = [
        lax.dynamic_index_in_dim(value, (me + steps) % count, 0, keepdims=False)
        for steps in range(count)
    ]
    others = [turned(parts[steps], axis, steps) for steps in range(1, count)]
    return functools.reduce(jnp.add, others, parts[0])


def all_sum(value, axis):
    others = [turned(value, axis, steps) for steps in range(1, lax.axis_size(axis))]
    return functools.reduce(jnp.add, others, value)


def collected(value, axis):
    others = [turned(value, axis, steps) for steps in range(1, lax.axis_size(axis))]
    return jnp.stack([value] + others)


def on_device(object_field, probe_modes, measured, offsets, live_slots):
    rows, cols = object_field.shape[1], object_field.shape[2]
    tables = tuple(jnp.asarray(table) for table in dft_tables(M))
    mid = rows // 2
    meta = jnp.concatenate(
        [
            offsets[0:1] - lax.axis_index(ROW) * rows,
            offsets[1:2] - lax.axis_index(COL) * cols,
            live_slots[None],
        ],
        axis=0,
    )
    first_cols, top_rows = run_cut(object_field, ((0, mid + M, M), (0, M, cols)))
    left_meta = shifted(meta, COL, 1) - jnp.array([[0], [cols], [0]], jnp.int32)
    wide_meta = jnp.concatenate([meta, left_meta], axis=1)
    upper_meta = shifted(wide_meta, ROW, 1) - jnp.array([[rows], [0], [0]], jnp.int32)
    (last_cols,) = run_cut(object_field, ((mid + M, M, M),), left_meta)
    first_cols = shifted(first_cols, COL, -1)
    last_cols = shifted(last_cols, COL, -1)
    lower = shifted(top_rows, ROW, -1)
    core, y, x = (lax.axis_index(axis) for axis in ("core", "y", "x"))
    mine = lax.dynamic_slice(
        probe_modes.reshape(4, M, M),
        (0, y * (M // 4) + x * PIECE, core * (M // 2)),
        (4, PIECE, M // 2),
    )
    common = (meta, core[None], measured, probe_modes, tables)

    plan = dict(
        name="left",
        region=(0, 0, rows + M, cols),
        rows=(0, rows),
        cols=(0, M),
        clear=[(0, 0, rows + M, cols)],
        outs=[
            (0, 0, rows, M, True),
            (0, M, mid + M, M, False),
            (mid + M, M, mid, M, False),
            (rows, 0, M, M, False),
        ],
        last=False,
    )
    left_own, upper_init, lower_init, below_left, sums = run_waves(
        plan,
        *common,
        [((0, 0, 0, 0, rows, cols), object_field), ((rows, 0, 0, 0, M, cols), lower)],
        [],
        after=(upper_meta,),
    )
    corner = shifted(gate(first_cols[:, :M], sums), ROW, -1)
    plan = dict(
        name="upper",
        region=(0, M, mid + M, cols),
        rows=(0, mid),
        cols=(M, cols),
        clear=[(0, M, mid + M, M)],
        outs=[
            (0, 0, mid, M, True),
            (0, M, M, M, False),
            (M, M, M, M, False),
            (mid, 0, M, cols, False),
        ],
        last=False,
    )
    upper_own, first_side, upper_side, middle, sums = run_waves(
        plan,
        *common,
        [
            ((0, 0, 0, M, mid + M, M), object_field),
            ((0, M, 0, 0, mid + M, M), first_cols),
        ],
        [((0, 0), upper_init)],
        before=sums,
    )
    plan = dict(
        name="lower",
        region=(mid, M, mid + M, cols),
        rows=(mid, rows),
        cols=(M, cols),
        clear=[(M, M, mid, M)],
        outs=[(0, 0, mid, M, True), (0, M, mid, M, False), (mid, 0, M, cols, False)],
        last=True,
    )
    lower_own, lower_side, below, kept, sent = run_waves(
        plan,
        *common,
        [
            ((0, 0, mid, M, mid, M), object_field),
            ((0, M, mid, 0, M, M), first_cols),
            ((M, M, 0, 0, M, M), last_cols),
            ((mid, 0, 0, M, M, M), lower),
            ((mid, M, 0, 0, M, M), corner),
        ],
        [((0, 0), middle), ((M, 0), lower_init)],
        before=sums,
        passed=(below_left,),
    )
    upper_side = shifted(upper_side, COL, 1)
    lower_side = shifted(lower_side, COL, 1)
    total = (kept + swapped(gate(sent, upper_side))).reshape(4, 4, 5, PIECE, M // 2)
    piece = scatter_sum(total, "y")
    below = shifted(gate(below, piece), ROW, 1)
    scale = run_light(
        jnp.concatenate([wide_meta, upper_meta], axis=1), probe_modes, piece, rows, cols
    )
    piece = scatter_sum(gate(piece, upper_side, lower_side, scale), "x")
    piece = all_sum(piece, "z")
    mine = mine - piece[:4] / jnp.sqrt(piece[4:5] + 1.0)
    strip = collected(mine, "x")
    first_side = shifted(gate(first_side + below[:, :, cols:], strip), COL, 1)
    strip = jnp.roll(strip[::-1], x + 1, axis=0)
    whole = collected(strip, "y")
    whole = gate(whole, first_side)
    new_probe = run_join(jnp.stack([y, core]), whole, swapped(whole))
    new_object = run_finish(
        object_field, left_own, upper_own, lower_own, first_side, upper_side, lower_side, below, scale
    )
    return (new_object, new_probe.reshape(probe_modes.shape))


def solution(mesh):
    grid = Mesh(mesh.devices.reshape(4, 2, 4, 4), ROW + COL)
    placed = (
        P(None, ROW, COL),
        P(),
        P(ROW + COL, None, None),
        P(None, ROW + COL),
        P(ROW + COL),
    )
    return jax.shard_map(
        on_device,
        mesh=grid,
        in_specs=placed,
        out_specs=(P(None, ROW, COL), P()),
        check_vma=False,
    )
```

```python
import functools
import math

import jax
import jax.numpy as jnp
import ml_dtypes
import numpy as np
from jax import lax
from jax.experimental import pallas as pl
from jax.experimental.pallas import tpu as pltpu
from jax.sharding import Mesh
from jax.sharding import PartitionSpec as P

M = 256
H = M // 2
ROOM = 56 * 1024 * 1024


def dft_tables(length):
    indices = np.arange(length)
    angles = (indices[:, None] * indices[None, :] % length) * (2.0 * math.pi / length)
    scale = 1.0 / math.sqrt(length)
    real = (np.cos(angles) * scale).astype(np.float32).astype(ml_dtypes.bfloat16)
    imag = (-np.sin(angles) * scale).astype(np.float32).astype(ml_dtypes.bfloat16)
    plain = np.block([[real, -imag], [imag, real]])
    conj = np.block([[real, imag], [-imag, real]])
    half = length // 2
    order = np.concatenate([np.arange(0, length, 2), np.arange(1, length, 2)])
    ahead = plain[np.concatenate([order, length + order])]
    back = []
    for first in range(2):
        re, im = real[:half, first::2], imag[:half, first::2]
        back.append(np.block([[re, im], [-im, re]]))
    return plain, conj, ahead, np.stack(back)


def shifted(value, axis, steps):
    count = lax.axis_size(axis)
    first, last = (max(0, -steps), min(count, count - steps))
    return lax.ppermute(value, axis, [(source, source + steps) for source in range(first, last)])


def shifted_both(value, steps):
    rows, cols = lax.axis_size(ROW), lax.axis_size(COL)
    pairs = []
    for r in range(rows):
        for c in range(cols):
            if 0 <= r + steps < rows and 0 <= c + steps < cols:
                pairs.append((r * cols + c, (r + steps) * cols + c + steps))
    return lax.ppermute(value, ROW + COL, pairs)


def cut_strip(ref, channel, row_base, row_rest, col_base, col_rest, rows):
    lane = lax.broadcasted_iota(jnp.int32, (rows + 8, 128), 1)
    keep = lane < 128 - col_rest
    turn = (128 - col_rest) & 127
    tiles = [
        pltpu.roll(ref[channel, pl.ds(row_base, rows + 8), pl.ds(col_base + 128 * t, 128)], turn, 1)
        for t in range(3)
    ]
    groups = rows // 8
    sub = lax.broadcasted_iota(jnp.int32, (groups, 8, 128), 1)
    keep_rows = sub < 8 - row_rest
    turn_rows = (8 - row_rest) & 7
    out = []
    for t in range(2):
        joined = jnp.where(keep, tiles[t], tiles[t + 1]).reshape(groups + 1, 8, 128)
        turned = pltpu.roll(joined, turn_rows, 1)
        out.append(jnp.where(keep_rows, turned[:groups], turned[1:]).reshape(rows, 128))
    return jnp.concatenate(out, axis=1)


def add_strip(ref, channel, row_base, row_rest, col_base, col_rest, value):
    rows = value.shape[0]
    groups = rows // 8
    sub = lax.broadcasted_iota(jnp.int32, (groups, 8, 128), 1)
    keep_rows = sub >= row_rest
    lane = lax.broadcasted_iota(jnp.int32, (rows + 8, 128), 1)
    keep = lane >= col_rest
    halves = []
    for t in range(2):
        turned = pltpu.roll(value[:, 128 * t : 128 * (t + 1)].reshape(groups, 8, 128), row_rest, 1)
        upper = jnp.where(keep_rows, turned, 0.0)
        lower = turned - upper
        zero = jnp.zeros((1, 8, 128), jnp.float32)
        full = jnp.concatenate([upper, zero], 0) + jnp.concatenate([zero, lower], 0)
        halves.append(pltpu.roll(full.reshape(rows + 8, 128), col_rest, 1))
    zero = jnp.zeros_like(halves[0])
    parts = [
        jnp.where(keep, halves[0], zero),
        jnp.where(keep, halves[1], halves[0]),
        jnp.where(keep, zero, halves[1]),
    ]
    for t in range(3):
        at = (channel, pl.ds(row_base, rows + 8), pl.ds(col_base + 128 * t, 128))
        ref[at] = ref[at] + parts[t]


def split_at(index, step):
    base = (index // step) * step
    return pl.multiple_of(base, step), index - base


STRIP = 64
PIECE = 16


def wave_kernel(plan, meta, core, measured, probe, plain, conj, split, back, *refs):
    loads, inits, outs = plan["loads"], plan["inits"], plan["outs"]
    row_at, col_at, height, width = plan["region"]
    refs = list(refs)

    def take(count):
        taken, refs[:] = refs[:count], refs[count:]
        return taken

    load_refs, init_refs = take(len(loads)), take(len(inits))
    before = take(1)[0] if plan["follows"] else None
    passed = take(plan["passed"])
    take(plan["after"])
    out_refs = take(len(outs))
    sum_refs = take(2 if plan["last"] else 1)
    order, ext, acc, meas, sums, patch, wave, half, far, in_sem, meas_sem, out_sem = refs
    slots = meta.shape[1]

    copies = []

    def copy_in(source, target):
        copy = pltpu.make_async_copy(source, target, in_sem.at[len(copies)])
        copies.append(copy)
        copy.start()

    for (r, c, top, start, h, w), ref in zip(loads, load_refs):
        copy_in(ref.at[:, top : top + h, start : start + w], ext.at[:, r : r + h, c : c + w])

    handed = [
        pltpu.make_async_copy(
            ref, out_refs[-1].at[:, :, : ref.shape[2]], out_sem.at[len(out_refs) + len(sum_refs) + at]
        )
        for at, ref in enumerate(passed)
    ]
    for copy in handed:
        copy.start()
    if before is not None:
        copy_in(before, sums)
    for (r, c), ref in zip(inits, init_refs):
        copy_in(ref, acc.at[:, r : r + ref.shape[1], c : c + ref.shape[2]])

    def fetch(slot):
        return [
            pltpu.make_async_copy(
                measured.at[slot, :, H * side : H * (side + 1)], meas.at[slot, side], meas_sem.at[slot, side]
            )
            for side in range(2)
        ]

    count = jnp.int32(0)
    for slot in range(slots):
        row, col, live = meta[0, slot], meta[1, slot], meta[2, slot]
        mine = (live > 0) & (row >= plan["rows"][0]) & (row < plan["rows"][1])
        mine = mine & (col >= plan["cols"][0]) & (col < plan["cols"][1])

        @pl.when(mine)
        def _(slot=slot, count=count):
            order[count] = slot
            for copy in fetch(slot):
                copy.start()

        count = count + mine.astype(jnp.int32)

    for r, c, h, w in plan["clear"]:

        def clear(at, carry, r=r, c=c, w=w):
            rows = pl.ds(pl.multiple_of(r + at * 32, 32), 32)
            acc[:, rows, c : c + w] = jnp.zeros((2, 32, w), jnp.float32)
            return carry

        lax.fori_loop(0, h // 32, clear, 0)
    if before is None:
        sums[...] = jnp.zeros_like(sums)
    for copy in copies:
        copy.wait()

    def left(use, table):
        for k in range(2):
            both = jnp.dot(table[...], wave[use, :, M * k : M * (k + 1)], preferred_element_type=jnp.float32)
            half[use, M * k : M * (k + 1), :M] = both[:M].astype(jnp.bfloat16)
            half[use, M * k : M * (k + 1), M:] = both[M:].astype(jnp.bfloat16)

    def left_back(use):
        for k in range(2):
            even, odd = (
                jnp.dot(
                    back[at],
                    wave[use, M * at : M * (at + 1), M * k : M * (k + 1)],
                    preferred_element_type=jnp.float32,
                )
                for at in range(2)
            )
            for side, both in enumerate((even + odd, even - odd)):
                for part in range(2):
                    half[use, M * k + H * side : M * k + H * (side + 1), M * part : M * (part + 1)] = both[
                        H * part : H * (part + 1)
                    ].astype(jnp.bfloat16)

    def right_mul(use, table):
        for part in range(2):
            far[use, :, M * part : M * (part + 1)] = jnp.dot(
                half[use], table[:, M * part : M * (part + 1)], preferred_element_type=jnp.float32
            )

    def add_sum(channel, at, value):
        for row in range(0, STRIP, PIECE):
            block = (at + row) // PIECE
            sums[0, block, channel] += value[row : row + PIECE, :128]
            sums[1, block, channel] += value[row : row + PIECE, 128:]

    def where(step):
        slot = order[step]
        row_base, row_rest = split_at(meta[0, slot] - row_at, 8)
        col_base, col_rest = split_at(meta[1, slot] - col_at, 128)
        return slot, row_base, row_rest, col_base, col_rest

    def cut(use, slot, row_base, row_rest, col_base, col_rest):
        for at in range(0, M, STRIP):
            rows = pl.ds(at, STRIP)
            base = pl.multiple_of(row_base + at, 8)
            o_re = cut_strip(ext, 0, base, row_rest, col_base, col_rest, STRIP)
            o_im = cut_strip(ext, 1, base, row_rest, col_base, col_rest, STRIP)
            patch[use, 0, rows, :] = o_re
            patch[use, 1, rows, :] = o_im
            add_sum(4, at, o_re * o_re + o_im * o_im)
            for k in range(2):
                p_re = probe[0, k, rows, :]
                p_im = probe[1, k, rows, :]
                cols = pl.ds(M * k, M)
                wave[use, rows, cols] = (p_re * o_re - p_im * o_im).astype(jnp.bfloat16)
                wave[use, pl.ds(M + at, STRIP), cols] = (p_re * o_im + p_im * o_re).astype(jnp.bfloat16)

    def resid(use, slot):
        for copy in fetch(slot):
            copy.wait()
        for at in range(0, M, STRIP):
            odd, start = at // H, at % H
            parts = [
                [far[use, pl.ds(M * k + at, STRIP), M * part : M * (part + 1)] for part in range(2)]
                for k in range(2)
            ]
            intensity = parts[0][0] * parts[0][0] + parts[0][1] * parts[0][1]
            intensity = intensity + parts[1][0] * parts[1][0] + parts[1][1] * parts[1][1]
            level = jnp.concatenate(
                [meas[slot, side, pl.ds(2 * start + odd, STRIP, 2), :] for side in range(2)], axis=1
            )
            factor = 1.0 - level * lax.rsqrt(level * jnp.maximum(intensity, 0.25))
            for k in range(2):
                for part in range(2):
                    wave[use, pl.ds(M * odd + H * part + start, STRIP), M * k : M * (k + 1)] = (
                        parts[k][part] * factor
                    ).astype(jnp.bfloat16)

    def grad(use, slot, row_base, row_rest, col_base, col_rest):
        for at in range(0, M, STRIP):
            rows = pl.ds(at, STRIP)
            base = pl.multiple_of(row_base + at, 8)
            o_re = patch[use, 0, rows, :]
            o_im = patch[use, 1, rows, :]
            g_re = None
            for k in range(2):
                n_re = far[use, pl.ds(M * k + at, STRIP), :M]
                n_im = far[use, pl.ds(M * k + at, STRIP), M:]
                p_re = probe[0, k, rows, :]
                p_im = probe[1, k, rows, :]
                add_sum(k, at, o_re * n_re + o_im * n_im)
                add_sum(2 + k, at, o_re * n_im - o_im * n_re)
                t_re = p_re * n_re + p_im * n_im
                t_im = p_re * n_im - p_im * n_re
                g_re, g_im = (t_re, t_im) if g_re is None else (g_re + t_re, g_im + t_im)
            add_strip(acc, 0, base, row_rest, col_base, col_rest, g_re)
            add_strip(acc, 1, base, row_rest, col_base, col_rest, g_im)

    def stages(use, step):
        at = where(step)
        return (
            lambda: cut(use, *at),
            lambda: left(use, split),
            lambda: right_mul(use, conj),
            lambda: resid(use, at[0]),
            lambda: left_back(use),
            lambda: right_mul(use, plain),
            lambda: grad(use, *at),
        )

    def visit_pair(pair, carry):
        first, second = stages(0, 2 * pair), stages(1, 2 * pair + 1)
        first[0]()
        for ahead, behind in zip(first[1:], second[:-1]):
            ahead()
            behind()
        second[-1]()
        return carry

    lax.fori_loop(0, count // 2, visit_pair, 0)

    @pl.when(count % 2 == 1)
    def _():
        for stage in stages(0, count - 1):
            stage()

    stores = []
    if plan["last"]:
        stores.append((sums.at[core[0]], sum_refs[0]))
        stores.append((sums.at[1 - core[0]], sum_refs[1]))
    else:
        stores.append((sums, sum_refs[0]))
    for (r, c, h, w, _), ref in zip(outs, out_refs):
        stores.append((acc.at[:, r : r + h, c : c + w], ref.at[:, :, ref.shape[2] - w :]))
    stores = [pltpu.make_async_copy(a, b, out_sem.at[i]) for i, (a, b) in enumerate(stores)]
    for copy in stores:
        copy.start()
    for copy in handed + stores:
        copy.wait()


def run_waves(plan, meta, core, measured, probe, tables, loads, inits, before=None, passed=(), after=()):
    slots = measured.shape[0]
    height, width = plan["region"][2:]
    f32 = jnp.float32
    plan = dict(
        plan,
        loads=[place for place, _ in loads],
        inits=[place for place, _ in inits],
        follows=before is not None,
        passed=len(passed),
        after=len(after),
    )
    anywhere = pl.BlockSpec(memory_space=pl.ANY)
    vmem = pl.BlockSpec(memory_space=pltpu.VMEM)
    smem = pl.BlockSpec(memory_space=pltpu.SMEM)
    arrays = [array for _, array in loads] + [array for _, array in inits]
    arrays = arrays + ([] if before is None else [before]) + list(passed) + list(after)
    in_hbm = pl.BlockSpec(memory_space=pltpu.HBM)
    array_specs = [in_hbm if array is loads[0][1] else anywhere for array in arrays]
    shapes = [jax.ShapeDtypeStruct((2, h, w), f32) for _, _, h, w, _ in plan["outs"]]
    out_specs = [in_hbm if stays else anywhere for *_, stays in plan["outs"]]
    for array in passed:
        shapes[-1] = jax.ShapeDtypeStruct((2, M, array.shape[2] + shapes[-1].shape[2]), f32)
    if plan["last"]:
        shapes = shapes + [jax.ShapeDtypeStruct((M // PIECE, 5, PIECE, M // 2), f32)] * 2
    else:
        shapes = shapes + [jax.ShapeDtypeStruct((2, M // PIECE, 5, PIECE, M // 2), f32)]
    return pl.pallas_call(
        functools.partial(wave_kernel, plan),
        out_shape=shapes,
        in_specs=[smem, smem, in_hbm] + [vmem] * 5 + array_specs,
        out_specs=out_specs + [anywhere] * (len(shapes) - len(out_specs)),
        scratch_shapes=[
            pltpu.SMEM((slots,), jnp.int32),
            pltpu.VMEM((2, height, width), f32),
            pltpu.VMEM((2, height, width), f32),
            pltpu.VMEM((slots, 2, M, H), f32),
            pltpu.VMEM((2, M // PIECE, 5, PIECE, M // 2), f32),
            pltpu.VMEM((2, 2, M, M), f32),
            pltpu.VMEM((2, 2 * M, 2 * M), jnp.bfloat16),
            pltpu.VMEM((2, 2 * M, 2 * M), jnp.bfloat16),
            pltpu.VMEM((2, 2 * M, 2 * M), f32),
            pltpu.SemaphoreType.DMA((len(arrays) + 1,)),
            pltpu.SemaphoreType.DMA((slots, 2)),
            pltpu.SemaphoreType.DMA((len(shapes) + 1,)),
        ],
        compiler_params=pltpu.CompilerParams(vmem_limit_bytes=34 * 1024 * 1024),
        cost_estimate=pl.CostEstimate(
            flops=10**8, bytes_accessed=2**20, transcendentals=0
        ),
        name=plan["name"],
    )(meta, core, measured, probe, *tables, *arrays)


def light_kernel(meta, probe, after, scale, light):
    slots = meta.shape[1]
    rows, cols = scale.shape
    light[...] = jnp.zeros_like(light)

    def visit(slot, carry):
        row, col = meta[0, slot], meta[1, slot]
        seen = (meta[2, slot] > 0) & (row > -M) & (row < rows) & (col > -M) & (col < cols)

        @pl.when(seen)
        def _():
            row_base, row_rest = split_at(row + M, 8)
            col_base, col_rest = split_at(col + M, 128)
            for at in range(0, M, STRIP):
                here = pl.ds(at, STRIP)
                value = probe[0, 0, here, :] * probe[0, 0, here, :]
                for part, k in ((1, 0), (0, 1), (1, 1)):
                    value = value + probe[part, k, here, :] * probe[part, k, here, :]
                base = pl.multiple_of(row_base + at, 8)
                add_strip(light, 0, base, row_rest, col_base, col_rest, value)

        return carry

    lax.fori_loop(0, slots, visit, 0)
    for at in range(0, rows, 64):
        scale[at : at + 64, :] = lax.rsqrt(light[0, M + at : M + at + 64, M : M + cols] + 1.0)


def run_light(meta, probe, after, rows, cols):
    return pl.pallas_call(
        light_kernel,
        out_shape=jax.ShapeDtypeStruct((rows, cols), jnp.float32),
        in_specs=[
            pl.BlockSpec(memory_space=pltpu.SMEM),
            pl.BlockSpec(memory_space=pltpu.VMEM),
            pl.BlockSpec(memory_space=pl.ANY),
        ],
        out_specs=pl.BlockSpec(memory_space=pltpu.VMEM),
        scratch_shapes=[pltpu.VMEM((1, rows + 2 * M, cols + 2 * M), jnp.float32)],
        compiler_params=pltpu.CompilerParams(vmem_limit_bytes=20 * 1024 * 1024),
        cost_estimate=pl.CostEstimate(flops=10**8, bytes_accessed=24 * 2**20, transcendentals=0),
        name="light",
    )(meta, probe, after)


def finish_kernel(
    tile, left_own, upper_own, lower_own, first_side, upper_side, lower_side, below, scale, out
):
    step = pl.program_id(0)
    factor = scale[...][None]

    def write(own, side):
        out[:, :, :M] = tile[:, :, :M] - (left_own[...] + side[...]) * factor[:, :, :M]
        out[:, :, M:] = tile[:, :, M:] - own[...] * factor[:, :, M:]

    @pl.when(step == 0)
    def _():
        write(upper_own, first_side)
        out[...] = out[...] - below[...] * factor

    @pl.when(step == 1)
    def _():
        write(upper_own, upper_side)

    @pl.when(step > 1)
    def _():
        write(lower_own, lower_side)


def run_finish(tile, left_own, upper_own, lower_own, first_side, upper_side, lower_side, below, scale):
    rows, cols = tile.shape[1], tile.shape[2]
    steps = rows // M
    half = steps // 2
    block = pl.BlockSpec((2, M, cols), lambda i: (0, i, 0))
    upper = pl.BlockSpec((2, M, M), lambda i: (0, jnp.minimum(i, half - 1), 0))
    lower = pl.BlockSpec((2, M, M), lambda i: (0, jnp.maximum(i - half, 0), 0))
    first = pl.BlockSpec((2, M, M), lambda i: (0, 0, 0))
    return pl.pallas_call(
        finish_kernel,
        grid=(steps,),
        out_shape=jax.ShapeDtypeStruct(tile.shape, jnp.float32),
        in_specs=[
            block,
            pl.BlockSpec((2, M, M), lambda i: (0, i, 0)),
            upper,
            lower,
            first,
            first,
            lower,
            pl.BlockSpec((2, M, cols), lambda i: (0, 0, 0)),
            pl.BlockSpec((M, cols), lambda i: (i, 0)),
        ],
        out_specs=block,
        compiler_params=pltpu.CompilerParams(vmem_limit_bytes=ROOM),
        cost_estimate=pl.CostEstimate(flops=10**7, bytes_accessed=20 * 2**20, transcendentals=0),
        name="finish",
    )(tile, left_own, upper_own, lower_own, first_side, upper_side, lower_side, below, scale)


def cut_kernel(pieces, after, tile, *refs):
    outs, sem = refs[after:-1], refs[-1]
    copies = [
        pltpu.make_async_copy(tile.at[:, r : r + h, :w], out, sem.at[i])
        for i, ((r, h, w), out) in enumerate(zip(pieces, outs))
    ]
    for copy in copies:
        copy.start()
    for copy in copies:
        copy.wait()


def run_cut(tile, pieces, *after, room=ROOM):
    anywhere = pl.BlockSpec(memory_space=pl.ANY)
    return pl.pallas_call(
        functools.partial(cut_kernel, pieces, len(after)),
        out_shape=[jax.ShapeDtypeStruct((2, h, w), jnp.float32) for _, h, w in pieces],
        in_specs=[anywhere] * (1 + len(after)),
        out_specs=[pl.BlockSpec(memory_space=pltpu.VMEM)] * len(pieces),
        scratch_shapes=[pltpu.SemaphoreType.DMA((len(pieces),))],
        compiler_params=pltpu.CompilerParams(vmem_limit_bytes=room),
        name="cut",
    )(tile, *after)


def join_kernel(place, mine, other, out):
    y = place[0]
    first = place[1] == 0
    for back in range(mine.shape[0]):
        for x in range(mine.shape[1]):
            row = ((y - back) & 3) * (M // 4) + x * PIECE
            rows = pl.ds(pl.multiple_of(row, PIECE), PIECE)
            for channel in range(4):
                a, b = mine[back, x, channel], other[back, x, channel]
                out[channel, rows, : M // 2] = jnp.where(first, a, b)
                out[channel, rows, M // 2 :] = jnp.where(first, b, a)


def run_join(place, mine, other):
    vmem = pl.BlockSpec(memory_space=pltpu.VMEM)
    return pl.pallas_call(
        join_kernel,
        out_shape=jax.ShapeDtypeStruct((4, M, M), jnp.float32),
        in_specs=[pl.BlockSpec(memory_space=pltpu.SMEM), vmem, vmem],
        out_specs=vmem,
        compiler_params=pltpu.CompilerParams(vmem_limit_bytes=8 * 1024 * 1024),
        name="join",
    )(place, mine, other)


def nothing(value, *rest):
    pass


def gate(value, *after):
    anywhere = pl.BlockSpec(memory_space=pl.ANY)
    return pl.pallas_call(
        nothing,
        out_shape=jax.ShapeDtypeStruct(value.shape, value.dtype),
        in_specs=[anywhere] * (1 + len(after)),
        out_specs=anywhere,
        input_output_aliases={0: 0},
        compiler_params=pltpu.CompilerParams(vmem_limit_bytes=2**20),
        name="gate",
    )(value, *after)


ROW, COL = ("y", "core"), ("x", "z")


def turned(value, axis, steps):
    count = lax.axis_size(axis)
    return lax.ppermute(value, axis, [(at, (at + steps) % count) for at in range(count)])


def swapped(value):
    return turned(value, "core", 1)


def scatter_sum(value, axis):
    count, me = lax.axis_size(axis), lax.axis_index(axis)
    parts = [
        lax.dynamic_index_in_dim(value, (me + steps) % count, 0, keepdims=False)
        for steps in range(count)
    ]
    others = [turned(parts[steps], axis, steps) for steps in range(1, count)]
    return functools.reduce(jnp.add, others, parts[0])


def all_sum(value, axis):
    others = [turned(value, axis, steps) for steps in range(1, lax.axis_size(axis))]
    return functools.reduce(jnp.add, others, value)


def collected(value, axis):
    others = [turned(value, axis, steps) for steps in range(1, lax.axis_size(axis))]
    return jnp.stack([value] + others)


def on_device(object_field, probe_modes, measured, offsets, live_slots):
    rows, cols = object_field.shape[1], object_field.shape[2]
    tables = tuple(jnp.asarray(table) for table in dft_tables(M))
    mid = rows // 2
    meta = jnp.concatenate(
        [
            offsets[0:1] - lax.axis_index(ROW) * rows,
            offsets[1:2] - lax.axis_index(COL) * cols,
            live_slots[None],
        ],
        axis=0,
    )
    first_cols, top_rows = run_cut(object_field, ((0, mid + M, M), (0, M, cols)))
    left_meta = shifted(meta, COL, 1) - jnp.array([[0], [cols], [0]], jnp.int32)
    wide_meta = jnp.concatenate([meta, left_meta], axis=1)
    upper_meta = shifted(wide_meta, ROW, 1) - jnp.array([[rows], [0], [0]], jnp.int32)
    (last_cols,) = run_cut(object_field, ((mid + M, M, M),), left_meta)
    first_cols = shifted(first_cols, COL, -1)
    last_cols = shifted(last_cols, COL, -1)
    lower = shifted(top_rows, ROW, -1)
    core, y, x = (lax.axis_index(axis) for axis in ("core", "y", "x"))
    mine = lax.dynamic_slice(
        probe_modes.reshape(4, M, M),
        (0, y * (M // 4) + x * PIECE, core * (M // 2)),
        (4, PIECE, M // 2),
    )
    common = (meta, core[None], measured, probe_modes, tables)

    plan = dict(
        name="left",
        region=(0, 0, rows + M, cols),
        rows=(0, rows),
        cols=(0, M),
        clear=[(0, 0, rows + M, cols)],
        outs=[
            (0, 0, rows, M, True),
            (0, M, mid + M, M, False),
            (mid + M, M, mid, M, False),
            (rows, 0, M, M, False),
        ],
        last=False,
    )
    left_own, upper_init, lower_init, below_left, sums = run_waves(
        plan,
        *common,
        [((0, 0, 0, 0, rows, cols), object_field), ((rows, 0, 0, 0, M, cols), lower)],
        [],
        after=(upper_meta,),
    )
    (corner,) = run_cut(first_cols, ((0, M, M),), sums, room=4 * 2**20)
    corner = shifted(corner, ROW, -1)
    plan = dict(
        name="upper",
        region=(0, M, mid + M, cols),
        rows=(0, mid),
        cols=(M, cols),
        clear=[(0, M, mid + M, M)],
        outs=[
            (0, 0, mid, M, True),
            (0, M, M, M, False),
            (M, M, M, M, False),
            (mid, 0, M, cols, False),
        ],
        last=False,
    )
    upper_own, first_side, upper_side, middle, sums = run_waves(
        plan,
        *common,
        [
            ((0, 0, 0, M, mid + M, M), object_field),
            ((0, M, 0, 0, mid + M, M), first_cols),
        ],
        [((0, 0), upper_init)],
        before=sums,
    )
    plan = dict(
        name="lower",
        region=(mid, M, mid + M, cols),
        rows=(mid, rows),
        cols=(M, cols),
        clear=[(M, M, mid, M)],
        outs=[(0, 0, mid, M, True), (0, M, mid, M, False), (mid, 0, M, cols, False)],
        last=True,
    )
    lower_own, lower_side, below, kept, sent = run_waves(
        plan,
        *common,
        [
            ((0, 0, mid, M, mid, M), object_field),
            ((0, M, mid, 0, M, M), first_cols),
            ((M, M, 0, 0, M, M), last_cols),
            ((mid, 0, 0, M, M, M), lower),
            ((mid, M, 0, 0, M, M), corner),
        ],
        [((0, 0), middle), ((M, 0), lower_init)],
        before=sums,
        passed=(below_left,),
    )
    upper_side = shifted(upper_side, COL, 1)
    lower_side = shifted(lower_side, COL, 1)
    total = (kept + swapped(gate(sent, upper_side))).reshape(4, 4, 5, PIECE, M // 2)
    piece = scatter_sum(total, "y")
    below = shifted(gate(below, piece), ROW, 1)
    scale = run_light(
        jnp.concatenate([wide_meta, upper_meta], axis=1), probe_modes, piece, rows, cols
    )
    piece = scatter_sum(gate(piece, upper_side, lower_side, scale), "x")
    piece = all_sum(piece, "z")
    mine = mine - piece[:4] / jnp.sqrt(piece[4:5] + 1.0)
    strip = collected(mine, "x")
    first_side = shifted(gate(first_side + below[:, :, cols:], strip), COL, 1)
    strip = jnp.roll(strip[::-1], x + 1, axis=0)
    whole = collected(strip, "y")
    whole = gate(whole, first_side)
    new_probe = run_join(jnp.stack([y, core]), whole, swapped(whole))
    new_object = run_finish(
        object_field, left_own, upper_own, lower_own, first_side, upper_side, lower_side, below, scale
    )
    return (new_object, new_probe.reshape(probe_modes.shape))


def solution(mesh):
    grid = Mesh(mesh.devices.reshape(4, 2, 4, 4), ROW + COL)
    placed = (
        P(None, ROW, COL),
        P(),
        P(ROW + COL, None, None),
        P(None, ROW + COL),
        P(ROW + COL),
    )
    return jax.shard_map(
        on_device,
        mesh=grid,
        in_specs=placed,
        out_specs=(P(None, ROW, COL), P()),
        check_vma=False,
    )
```
